128 devices in a mesh: rep: 8 (over x, core), shard: 16 (over z, y).
Axes of the slice: x: 4, y: 4, z: 4, core: 2. Of those that a mesh axis runs over, the one named last changes fastest.
Arguments:
- inputs: bfloat16 [32768, 960], P(('rep', 'shard')), may hold values from -6 to 6
- seg_ids: int32 [32768], P(('rep', 'shard')), may hold values from 0 to 32767, as said below
- cotangent: bfloat16 [32768, 960], P(('rep', 'shard')), may hold values from -6 to 6
- w_query: bfloat16 [960, 960], P('shard'), may hold values from -0.1613743 to 0.1613743
- w_key: bfloat16 [960, 320], P('shard'), may hold values from -0.1613743 to 0.1613743
- w_value: bfloat16 [960, 320], P('shard'), may hold values from -0.1875 to 0.1875
- w_output: bfloat16 [960, 960], P('shard'), may hold values from -0.5 to 0.5
- w_gate: bfloat16 [960, 2560], P('shard'), may hold values from -0.1875 to 0.1875
- w_up: bfloat16 [960, 2560], P('shard'), may hold values from -0.1875 to 0.1875
- w_down: bfloat16 [2560, 960], P('shard'), may hold values from -0.125 to 0.125
- gain_attn: float32 [960], P('shard'), may hold values from 0.5 to 1.5
- gain_ffn: float32 [960], P('shard'), may hold values from 0.1 to 1.9
Outputs:
- outputs: bfloat16 [32768, 960], P(('rep', 'shard'))
- grad_inputs: bfloat16 [32768, 960], P(('rep', 'shard'))
- grad_query: float32 [960, 960], P('shard')
- grad_key: float32 [960, 320], P('shard')
- grad_value: float32 [960, 320], P('shard')
- grad_output: float32 [960, 960], P('shard')
- grad_gate: float32 [960, 2560], P('shard')
- grad_up: float32 [960, 2560], P('shard')
- grad_down: float32 [2560, 960], P('shard')
- grad_gain_attn: float32 [960], P('shard')
- grad_gain_ffn: float32 [960], P('shard')
The draws below stay inside these ranges and needn't reach their ends.
Inputs may be any that keep to these rules, and one draw needn't show every extreme that they name: `seg_ids`: ids never fall within one device's 256 slots, each device's slots begin a new sequence, and no id is found on two devices; in every draw one device holds a single sequence of 256 tokens.
All inputs are finite; a program needn't handle non-finite values.
Results may differ from the reference program's by a relative error of at most 0.04.
Values may be sent and summed in bfloat16 or wider, within the bound.
No kernel may reach another device: no remote copies, remote signals or barrier semaphores. Data moves between devices by JAX's collectives and lax.ppermute only.
A program may use at most 128 MiB of HBM per device.

```python
import jax
import jax.numpy as jnp
from jax import lax

D = 960
H = 15
KVH = 5
FF = 2560
TOK_DEV = 256
QW = 960
KW = 320
TOKENS = 32768


def draw_seg_ids(key, part):
    blocks = TOKENS // TOK_DEV
    key_rate, key_cut, key_one = jax.random.split(jax.random.fold_in(key, 17), 3)
    cut_rate = jax.random.randint(key_rate, (blocks, 1), 1, 33)
    boundary = jax.random.randint(key_cut, (blocks, TOK_DEV), 0, 256) < cut_rate
    single = jax.random.randint(key_one, (), 0, blocks)
    block_index = jnp.arange(blocks, dtype=jnp.int32)[:, None]
    position = jnp.arange(TOK_DEV, dtype=jnp.int32)[None, :]
    boundary = boundary & (block_index != single) | (position == 0)
    local = jnp.cumsum(boundary.astype(jnp.int32), axis=1) - 1
    shift_last = jnp.where(block_index == blocks - 1, TOK_DEV - 1 - local[:, -1:], 0)
    return (block_index * TOK_DEV + local + shift_last).reshape(TOKENS).astype(jnp.int32)


def draw_inputs(key, part):
    private = jax.random.fold_in(key, 53)
    entries = jnp.clip(jax.random.normal(private, (TOKENS, D), jnp.float32), -6.0, 6.0)
    return entries.astype(jnp.bfloat16)


def draw_entries(key, columns_count, seed_shift):
    private = jax.random.fold_in(key, seed_shift)
    factor = D ** (-0.5)
    entries = jnp.clip(jax.random.normal(private, (D, columns_count), jnp.float32), -4.0, 4.0)
    return (entries * factor).astype(jnp.bfloat16)


def draw_w_query(key, part):
    return draw_entries(key, QW, 41)


def draw_w_key(key, part):
    return draw_entries(key, KW, 43)


def shard_levels(own_key, dims, shards, smallest, largest):
    def one(axis_at, blocks):
        draws = jax.random.uniform(jax.random.fold_in(jax.random.fold_in(own_key, 6), axis_at), (blocks,), jnp.float32, smallest / len(shards), largest / len(shards))
        return jnp.repeat(jnp.exp(draws), dims[axis_at] // blocks).reshape((-1,) + (1,) * (len(dims) - axis_at - 1))

    level = one(*shards[0])
    for cut in shards[1:]:
        level = level * one(*cut)
    return level


def bell_draw(own_key, extent, deviation, bound, cuts=(), held_as=jnp.bfloat16):
    array = deviation * jax.random.normal(own_key, extent, jnp.float32)
    if cuts:
        array = array * shard_levels(own_key, extent, cuts, -0.22, 0.18)
    return jnp.clip(array, -bound, bound).astype(held_as)


def setup_inputs(seed: int = 0) -> dict:
    streams_of = jax.random.split(jax.random.key(seed), 13)
    return {
        "inputs": draw_inputs(jax.random.fold_in(streams_of[12], 71), 0),
        "seg_ids": draw_seg_ids(jax.random.fold_in(streams_of[12], 71), 0),
        "cotangent": bell_draw(streams_of[2], (TOKENS, D), 1.0, 6.0, ((0, 128),)),
        "w_query": draw_w_query(jax.random.fold_in(streams_of[12], 71), 0),
        "w_key": draw_w_key(jax.random.fold_in(streams_of[12], 71), 0),
        "w_value": bell_draw(streams_of[5], (D, KW), D ** -0.5, 0.1875, ((0, 16),)),
        "w_output": bell_draw(streams_of[6], (QW, D), (QW // 8) ** -0.5, 0.5, ((0, 16),)),
        "w_gate": bell_draw(streams_of[7], (D, FF), D ** -0.5, 0.1875, ((0, 16),)),
        "w_up": bell_draw(streams_of[8], (D, FF), D ** -0.5, 0.1875, ((0, 16),)),
        "w_down": bell_draw(streams_of[9], (FF, D), FF ** -0.5, 0.125, ((0, 16),)),
        "gain_attn": jnp.clip(1.0 + 0.1 * jax.random.normal(streams_of[10], (D,), jnp.float32), 0.5, 1.5),
        "gain_ffn": jnp.clip(1.0 + 0.18 * jax.random.normal(streams_of[11], (D,), jnp.float32), 0.1, 1.9),
    }


EPSILON = 1e-05
THETA = 100000.0

def mult(form, left, right):
    return jnp.einsum(form, left.astype(jnp.float32), right.astype(jnp.float32))

def rms_forward(values, gain):
    scale = lax.rsqrt(lax.optimization_barrier(jnp.mean(values * values, axis=-1, keepdims=True)) + EPSILON)
    normed = values * scale
    return (normed, scale, (normed * gain).astype(jnp.bfloat16))

def rms_backward(grad_out, normed, scale, gain):
    grad_norm = grad_out * gain
    grad_in = scale * (grad_norm - normed * lax.optimization_barrier(jnp.mean(grad_norm * normed, axis=-1, keepdims=True)))
    return (grad_in, lax.optimization_barrier(jnp.sum(grad_out * normed, axis=0)))

def rotary_tables(segments, head_dim):
    count = segments.shape[-1]
    index = jnp.arange(count, dtype=jnp.int32)
    same = segments[:, :, None] == segments[:, None, :]
    first = lax.optimization_barrier(jnp.min(jnp.where(same, index, count), axis=-1))
    position = (index - first).astype(jnp.float32)
    half = head_dim // 2
    freq = THETA ** (-jnp.arange(half, dtype=jnp.float32) / half)
    angle = position[..., None] * freq
    return (jnp.cos(angle), jnp.sin(angle))

def rotate(values, cos_table, sin_table):
    half = values.shape[-1] // 2
    first, second = (values[..., :half], values[..., half:])
    cos_part = cos_table[:, :, None, :]
    sin_part = sin_table[:, :, None, :]
    return jnp.concatenate([first * cos_part - second * sin_part, second * cos_part + first * sin_part], axis=-1)

def unrotate(values, cos_table, sin_table):
    half = values.shape[-1] // 2
    first, second = (values[..., :half], values[..., half:])
    cos_part = cos_table[:, :, None, :]
    sin_part = sin_table[:, :, None, :]
    return jnp.concatenate([first * cos_part + second * sin_part, second * cos_part - first * sin_part], axis=-1)

def attention_probs(query_rot, key_rot, allowed, log_total):
    scores = mult('bqkgd,btkd->bkgqt', query_rot, key_rot) * 0.125
    return jnp.where(allowed, jnp.exp(scores - log_total), 0.0)

def forward(inputs, segments, weights, heads, kv_heads):
    w_query, w_key, w_value, w_output, w_gate, w_up, w_down, gain_attn, gain_ffn = weights
    batch, count = segments.shape
    rows = inputs.shape[0]
    head_dim = w_query.shape[1] // heads
    group = heads // kv_heads
    xfloat = inputs.astype(jnp.float32)
    normed_one, scale_one, hidden_one = rms_forward(xfloat, gain_attn)
    cos_table, sin_table = rotary_tables(segments, head_dim)
    query = jnp.dot(hidden_one, w_query, preferred_element_type=jnp.float32).reshape(batch, count, heads, head_dim)
    keys = jnp.dot(hidden_one, w_key, preferred_element_type=jnp.float32).reshape(batch, count, kv_heads, head_dim)
    values = jnp.dot(hidden_one, w_value, preferred_element_type=jnp.float32).astype(jnp.bfloat16)
    values = values.reshape(batch, count, kv_heads, head_dim)
    query_rot = rotate(query, cos_table, sin_table).astype(jnp.bfloat16).reshape(batch, count, kv_heads, group, head_dim)
    key_rot = rotate(keys, cos_table, sin_table).astype(jnp.bfloat16)
    index = jnp.arange(count, dtype=jnp.int32)
    allowed = (segments[:, :, None] == segments[:, None, :]) & (index[:, None] >= index[None, :])
    allowed = allowed[:, None, None]
    scores = mult('bqkgd,btkd->bkgqt', query_rot, key_rot) * 0.125
    row_max = lax.optimization_barrier(jnp.max(jnp.where(allowed, scores, -1e+30), axis=-1, keepdims=True))
    log_total = row_max + jnp.log(lax.optimization_barrier(jnp.sum(jnp.where(allowed, jnp.exp(scores - row_max), 0.0), axis=-1, keepdims=True)))
    probs = jnp.where(allowed, jnp.exp(scores - log_total), 0.0)
    probs_low = probs.astype(jnp.bfloat16)
    attended = mult('bkgqt,btkd->bqkgd', probs_low, values).astype(jnp.bfloat16).reshape(rows, heads * head_dim)
    mixed = xfloat + jnp.dot(attended, w_output, preferred_element_type=jnp.float32)
    normed_two, scale_two, hidden_two = rms_forward(mixed, gain_ffn)
    gate = jnp.dot(hidden_two, w_gate, preferred_element_type=jnp.float32)
    up_proj = jnp.dot(hidden_two, w_up, preferred_element_type=jnp.float32)
    sigmoid_gate = jax.nn.sigmoid(gate)
    activ = (gate * sigmoid_gate * up_proj).astype(jnp.bfloat16)
    result = (mixed + jnp.dot(activ, w_down, preferred_element_type=jnp.float32)).astype(jnp.bfloat16)
    saved = {'normed_one': normed_one, 'scale_one': scale_one, 'hidden_one': hidden_one, 'cos': cos_table, 'sin': sin_table, 'query_rot': query_rot, 'key_rot': key_rot, 'values': values, 'allowed': allowed, 'log_total': log_total, 'attended': attended, 'normed_two': normed_two, 'scale_two': scale_two, 'hidden_two': hidden_two, 'gate': gate, 'up_proj': up_proj, 'activ': activ}
    return (saved, result)

def backward_ffn(saved, cotangent, weights):
    w_gate, w_up, w_down, gain_ffn = (weights[4], weights[5], weights[6], weights[8])
    gate, up_proj, hidden_two = (saved['gate'], saved['up_proj'], saved['hidden_two'])
    grad_down = jnp.dot(saved['activ'].T, cotangent, preferred_element_type=jnp.float32)
    d_act = jnp.dot(cotangent, w_down.T, preferred_element_type=jnp.float32)
    sigmoid_gate = jax.nn.sigmoid(gate)
    d_gate = (d_act * up_proj * sigmoid_gate * (1.0 + gate * (1.0 - sigmoid_gate))).astype(jnp.bfloat16)
    d_up = (d_act * gate * sigmoid_gate).astype(jnp.bfloat16)
    grad_gate = jnp.dot(hidden_two.T, d_gate, preferred_element_type=jnp.float32)
    grad_up = jnp.dot(hidden_two.T, d_up, preferred_element_type=jnp.float32)
    d_hidden = jnp.dot(d_gate, w_gate.T, preferred_element_type=jnp.float32)
    d_hidden = d_hidden + jnp.dot(d_up, w_up.T, preferred_element_type=jnp.float32)
    d_normed, grad_gain_ffn = rms_backward(d_hidden, saved['normed_two'], saved['scale_two'], gain_ffn)
    d_mixed = cotangent.astype(jnp.float32) + d_normed
    return (d_mixed, (grad_gate, grad_up, grad_down, grad_gain_ffn))

def backward_attn(saved, d_mixed, weights):
    w_query, w_key, w_value, w_output, gain_attn = (weights[0], weights[1], weights[2], weights[3], weights[7])
    query_rot, key_rot, values = (saved['query_rot'], saved['key_rot'], saved['values'])
    batch, count, kv_heads, group, head_dim = query_rot.shape
    rows = batch * count
    d_attn = d_mixed.astype(jnp.bfloat16)
    grad_output = jnp.dot(saved['attended'].T, d_attn, preferred_element_type=jnp.float32)
    d_out = jnp.dot(d_attn, w_output.T, preferred_element_type=jnp.float32).astype(jnp.bfloat16)
    d_out = d_out.reshape(batch, count, kv_heads, group, head_dim)
    probs = attention_probs(query_rot, key_rot, saved['allowed'], saved['log_total'])
    probs_low = probs.astype(jnp.bfloat16)
    d_vals = mult('bkgqt,bqkgd->btkd', probs_low, d_out)
    d_probs = mult('bqkgd,btkd->bkgqt', d_out, values)
    row_dot = lax.optimization_barrier(jnp.sum(probs * d_probs, axis=-1, keepdims=True))
    d_scores = (probs * (d_probs - row_dot) * 0.125).astype(jnp.bfloat16)
    d_query = mult('bkgqt,btkd->bqkgd', d_scores, key_rot).reshape(batch, count, kv_heads * group, head_dim)
    d_keys = mult('bkgqt,bqkgd->btkd', d_scores, query_rot)
    d_query = unrotate(d_query, saved['cos'], saved['sin']).astype(jnp.bfloat16).reshape(rows, -1)
    d_keys = unrotate(d_keys, saved['cos'], saved['sin']).astype(jnp.bfloat16).reshape(rows, -1)
    d_vals = d_vals.astype(jnp.bfloat16).reshape(rows, -1)
    hidden_one = saved['hidden_one']
    grad_query = jnp.dot(hidden_one.T, d_query, preferred_element_type=jnp.float32)
    grad_key = jnp.dot(hidden_one.T, d_keys, preferred_element_type=jnp.float32)
    grad_value = jnp.dot(hidden_one.T, d_vals, preferred_element_type=jnp.float32)
    d_hidden = jnp.dot(d_query, w_query.T, preferred_element_type=jnp.float32)
    d_hidden = d_hidden + jnp.dot(d_keys, w_key.T, preferred_element_type=jnp.float32)
    d_hidden = d_hidden + jnp.dot(d_vals, w_value.T, preferred_element_type=jnp.float32)
    d_normed, grad_gain_attn = rms_backward(d_hidden, saved['normed_one'], saved['scale_one'], gain_attn)
    grad_in = (d_mixed + d_normed).astype(jnp.bfloat16)
    return (grad_in, (grad_query, grad_key, grad_value, grad_output, grad_gain_attn))

def reference(inputs, seg_ids, cotangent, w_query, w_key, w_value, w_output, w_gate, w_up, w_down, gain_attn, gain_ffn):
    weights = (w_query, w_key, w_value, w_output, w_gate, w_up, w_down, gain_attn, gain_ffn)
    per_block = 16
    blocks = TOKENS // (per_block * TOK_DEV)
    rows = per_block * TOK_DEV
    x_all = inputs.reshape(blocks, rows, D)
    seg_all = seg_ids.reshape(blocks, per_block, TOK_DEV)
    dy_all = cotangent.reshape(blocks, rows, D)
    zeros = tuple((jnp.zeros(weight.shape, jnp.float32) for weight in weights))

    def advance(totals, item):
        x_rows, seg_rows, dy_rows = item
        saved, result = forward(x_rows, seg_rows, weights, H, KVH)
        d_mixed, ffn_grads = backward_ffn(saved, dy_rows, weights)
        grad_in, attn_grads = backward_attn(saved, d_mixed, weights)
        grads = attn_grads[:4] + ffn_grads[:3] + (attn_grads[4], ffn_grads[3])
        return (tuple((total + grad for total, grad in zip(totals, grads))), (result, grad_in))
    totals, (results, grads_in) = lax.scan(advance, zeros, (x_all, seg_all, dy_all))
    return (results.reshape(TOKENS, D), grads_in.reshape(TOKENS, D), totals[0], totals[1], totals[2], totals[3], totals[4], totals[5], totals[6], totals[7], totals[8])
```

```python
import jax
import jax.numpy as jnp
from jax import lax
from jax.sharding import PartitionSpec as P

H = 15
KVH = 5
HD = 64
D = 960
QK = 1280
FF = 2560
EPSILON = 1e-05
THETA = 100000.0
F32 = jnp.float32
BF = jnp.bfloat16
AX = ("rep", "shard")


def device(x, c, z, y):
    return ((x % 4) * 2 + c % 2) * 16 + (z % 4) * 4 + y % 4


def shift(value, axis, step):
    move = {"x": 0, "c": 0, "z": 0, "y": 0, axis: step}
    pairs = [
        (device(x, c, z, y), device(x + move["x"], c + move["c"], z + move["z"], y + move["y"]))
        for x in range(4)
        for c in range(2)
        for z in range(4)
        for y in range(4)
    ]
    return lax.ppermute(value, AX, pairs)


def dot(left, right):
    return jnp.dot(left, right, preferred_element_type=F32)


def dot_t(left, right):
    return lax.dot_general(left, right, (((1,), (1,)), ((), ())), preferred_element_type=F32)


def t_dot(left, right):
    return lax.dot_general(left, right, (((0,), (0,)), ((), ())), preferred_element_type=F32)


def collect(value, axis):
    return [value] + [shift(value, axis, -step) for step in (1, 2, 3)]


def spread(blocks, axis):
    got = [shift(blocks[step], axis, step) for step in (1, 2, 3)]
    total = blocks[0].astype(F32)
    for part in got:
        total = total + part.astype(F32)
    return total.astype(BF)


def gather_rel(value, first, second):
    inner = jnp.concatenate(collect(value, first), axis=0)
    mine = jnp.concatenate(collect(inner, second), axis=0)
    return jnp.concatenate([mine, shift(mine, "c", 1)], axis=0)


def gather_abs(value, first, second, where):
    rows, cols = value.shape
    inner = jnp.zeros((4, rows, cols), BF)
    for step, part in enumerate(collect(value, first)):
        inner = lax.dynamic_update_slice(inner, part[None], ((where[first] + step) % 4, 0, 0))
    mine = jnp.zeros((4, 4, rows, cols), BF)
    for step, part in enumerate(collect(inner, second)):
        at = (where[second] + step) % 4
        if second == "z":
            mine = lax.dynamic_update_slice(mine, part[None], (at, 0, 0, 0))
        else:
            mine = lax.dynamic_update_slice(mine, part[:, None], (0, at, 0, 0))
    other = shift(mine, "c", 1)
    low = where["c"] == 0
    both = jnp.stack([jnp.where(low, mine, other), jnp.where(low, other, mine)], axis=2)
    return both.reshape(32 * rows, cols)


def scatter_rel(own, other, first, second):
    total = (own + shift(other.astype(BF), "c", 1).astype(F32)).astype(BF)
    cols = total.shape[1]
    total = total.reshape(4, -1, cols)
    total = spread([total[i] for i in range(4)], first)
    total = total.reshape(4, -1, cols)
    return spread([total[i] for i in range(4)], second)


def scatter_abs(value, first, second, where):
    rows = value.shape[0] // 32
    cols = value.shape[1]
    value = value.reshape(4, 4, 2, rows, cols)
    own = lax.dynamic_index_in_dim(value, where["c"], 2, keepdims=False)
    other = lax.dynamic_index_in_dim(value, 1 - where["c"], 2, keepdims=False)
    total = (own.astype(F32) + shift(other, "c", 1).astype(F32)).astype(BF)
    dim = 0 if first == "z" else 1
    total = spread(
        [
            lax.dynamic_index_in_dim(total, (where[first] + i) % 4, dim, keepdims=False)
            for i in range(4)
        ],
        first,
    )
    return spread(
        [
            lax.dynamic_index_in_dim(total, (where[second] + i) % 4, 0, keepdims=False)
            for i in range(4)
        ],
        second,
    )


def finish(part, where):
    one, two, three = [shift(part, "x", step) for step in (1, 2, 3)]
    total = (part.astype(F32) + two.astype(F32)) + (one.astype(F32) + three.astype(F32))
    total = total.astype(BF)
    other = shift(total, "c", 1)
    low = where["c"] == 0
    return jnp.concatenate(
        [jnp.where(low, total, other), jnp.where(low, other, total)], axis=0
    ).astype(F32)


def order_matrix(where, major, minor):
    place = lax.broadcasted_iota(jnp.int32, (D, 1024), 1)
    natural = lax.broadcasted_iota(jnp.int32, (D, 1024), 0)
    core = (where["c"] + place // 512) % 2
    at = {
        major: (where[major] + (place // 128) % 4) % 4,
        minor: (where[minor] + (place // 32) % 4) % 4,
    }
    inner = core * 32 + place % 32
    target = (at["z"] * 4 + at["y"]) * 60 + inner
    return ((target == natural) & (inner < 60)).astype(BF)


def rotary_tables(segments):
    count = segments.shape[0]
    index = jnp.arange(count, dtype=jnp.int32)
    same = segments[:, None] == segments[None, :]
    first = jnp.min(jnp.where(same, index[None, :], count), axis=-1)
    position = (index - first).astype(F32)
    half = HD // 2
    freq = THETA ** (-jnp.arange(half, dtype=F32) / half)
    angle = position[:, None] * freq
    return (jnp.cos(angle)[:, None, :], jnp.sin(angle)[:, None, :])


def rotate(values, cos, sin):
    a, b = (values[..., : HD // 2], values[..., HD // 2 :])
    return jnp.concatenate([a * cos - b * sin, b * cos + a * sin], axis=-1)


def unrotate(values, cos, sin):
    a, b = (values[..., : HD // 2], values[..., HD // 2 :])
    return jnp.concatenate([a * cos + b * sin, b * cos - a * sin], axis=-1)


def mult(form, left, right):
    return jnp.einsum(form, left, right, preferred_element_type=F32)


def norm(values):
    scale = lax.rsqrt(jnp.mean(values * values, axis=-1, keepdims=True) + EPSILON)
    return (values * scale, scale)


def norm_back(e, normed, scale):
    return scale * (e - normed * jnp.mean(e * normed, axis=-1, keepdims=True))


def half_rows(value, where):
    padded = jnp.pad(value, ((0, 4), (0, 0)))
    return lax.dynamic_slice_in_dim(padded, where["c"] * 32, 32, 0)


def local(x, seg, dy, wq, wk, wv, wo, wg, wu, wd, gain_a, gain_f):
    rep = lax.axis_index("rep")
    shard = lax.axis_index("shard")
    where = {"c": rep % 2, "z": shard // 4, "y": shard % 4}
    ga = gain_a[:, None]
    gf = gain_f[:, None]
    scaled = lambda w, g: (w.astype(F32) * g).astype(BF)
    s_qk = half_rows(jnp.concatenate([scaled(wq, ga), scaled(wk, ga)], axis=1), where)
    s_ov = half_rows(jnp.concatenate([wo, scaled(wv, ga)], axis=1), where)
    s_g = half_rows(scaled(wg, gf), where)
    s_u = half_rows(scaled(wu, gf), where)
    s_d = lax.dynamic_slice_in_dim(wd, where["c"] * 80, 80, 0)
    w_qk = gather_rel(s_qk, "y", "z")
    w_ov = gather_rel(s_ov, "z", "y")
    w_g = gather_rel(s_g, "y", "z")
    w_u = gather_rel(s_u, "z", "y")
    w_d1 = gather_abs(s_d[:, :512], "y", "z", where)
    w_d2 = gather_abs(s_d[:, 512:], "z", "y", where)
    e1 = order_matrix(where, "z", "y")
    e2 = order_matrix(where, "y", "z")

    xf = x.astype(F32)
    n1, r1 = norm(xf)
    h1 = n1.astype(BF)
    h1a = dot(h1, e1).astype(BF)
    h1b = dot(h1, e2).astype(BF)
    cos, sin = rotary_tables(seg)
    qk = dot(h1a, w_qk)
    values = dot(h1b, w_ov)[:, D:].astype(BF).reshape(256, KVH, HD)
    qr = rotate(qk[:, :D].reshape(256, H, HD), cos, sin).astype(BF).reshape(256, KVH, 3, HD)
    kr = rotate(qk[:, D:].reshape(256, KVH, HD), cos, sin).astype(BF)
    index = jnp.arange(256, dtype=jnp.int32)
    allowed = (seg[:, None] == seg[None, :]) & (index[:, None] >= index[None, :])
    allowed = allowed[None, None]
    scores = mult("qkgd,tkd->kgqt", qr, kr) * 0.125
    row_max = jnp.max(jnp.where(allowed, scores, -1e30), axis=-1, keepdims=True)
    weight = jnp.where(allowed, jnp.exp(scores - row_max), 0.0)
    probs = weight / jnp.sum(weight, axis=-1, keepdims=True)
    pb = probs.astype(BF)
    att = mult("kgqt,tkd->qkgd", pb, values).astype(BF).reshape(256, D)
    att_b = dot(att, e2).astype(BF)
    w_o = w_ov[:, :D]
    mixed = xf + dot(att_b, w_o)

    n2, r2 = norm(mixed)
    h2 = n2.astype(BF)
    h2a = dot(h2, e1).astype(BF)
    h2b = dot(h2, e2).astype(BF)
    gate = dot(h2a, w_g)
    up = dot(h2b, w_u)
    sig = jax.nn.sigmoid(gate)
    act = (gate * sig * up).astype(BF)
    out = jnp.concatenate(
        [mixed[:, :512] + dot(act, w_d1), mixed[:, 512:] + dot(act, w_d2)], axis=1
    ).astype(BF)

    g_d1 = t_dot(act, dy[:, :512]).astype(BF)
    g_d2 = t_dot(act, dy[:, 512:]).astype(BF)
    t_d1 = finish(scatter_abs(g_d1, "z", "y", where), where)
    t_d2 = finish(scatter_abs(g_d2, "y", "z", where), where)
    d_act = dot_t(dy[:, :512], w_d1) + dot_t(dy[:, 512:], w_d2)
    d_gate = (d_act * up * sig * (1.0 + gate * (1.0 - sig))).astype(BF)
    d_up = (d_act * gate * sig).astype(BF)
    t_g = finish(
        scatter_rel(t_dot(h2a[:, :512], d_gate), t_dot(h2a[:, 512:], d_gate), "z", "y"), where
    )
    t_u = finish(
        scatter_rel(t_dot(h2b[:, :512], d_up), t_dot(h2b[:, 512:], d_up), "y", "z"), where
    )
    e_f = dot_t(dot_t(d_gate, w_g).astype(BF), e1) + dot_t(dot_t(d_up, w_u).astype(BF), e2)
    d_mixed = dy.astype(F32) + norm_back(e_f, n2, r2)

    d_attn = d_mixed.astype(BF)
    d_ob = dot_t(dot_t(d_attn, w_o).astype(BF), e2).astype(BF).reshape(256, KVH, 3, HD)
    d_vals = mult("kgqt,qkgd->tkd", pb, d_ob)
    d_p = mult("qkgd,tkd->kgqt", d_ob, values)
    row_dot = jnp.sum(probs * d_p, axis=-1, keepdims=True)
    d_s = (probs * (d_p - row_dot) * 0.125).astype(BF)
    d_q = mult("kgqt,tkd->qkgd", d_s, kr).reshape(256, H, HD)
    d_k = mult("kgqt,qkgd->tkd", d_s, qr)
    d_qk = jnp.concatenate(
        [
            unrotate(d_q, cos, sin).astype(BF).reshape(256, D),
            unrotate(d_k, cos, sin).astype(BF).reshape(256, 320),
        ],
        axis=1,
    )
    d_v = d_vals.astype(BF).reshape(256, 320)
    t_qk = finish(
        scatter_rel(t_dot(h1a[:, :512], d_qk), t_dot(h1a[:, 512:], d_qk), "z", "y"), where
    )
    g_ov = [
        jnp.concatenate([t_dot(att_b[:, s], d_attn), t_dot(h1b[:, s], d_v)], axis=1)
        for s in (slice(0, 512), slice(512, 1024))
    ]
    t_ov = finish(scatter_rel(g_ov[0], g_ov[1], "y", "z"), where)
    d_v_wide = jnp.pad(d_v, ((0, 0), (D, 0)))
    e_a = dot_t(dot_t(d_qk, w_qk).astype(BF), e1) + dot_t(dot_t(d_v_wide, w_ov).astype(BF), e2)
    grad_in = (d_mixed + norm_back(e_a, n1, r1)).astype(BF)

    t_qk, t_ov, t_g, t_u = (t_qk[:60], t_ov[:60], t_g[:60], t_u[:60])
    t_q, t_k, t_o, t_v = (t_qk[:, :D], t_qk[:, D:], t_ov[:, :D], t_ov[:, D:])
    rowsum = lambda w, t: jnp.sum(w.astype(F32) * t, axis=1)
    grad_ga = rowsum(wq, t_q) + rowsum(wk, t_k) + rowsum(wv, t_v)
    grad_gf = rowsum(wg, t_g) + rowsum(wu, t_u)
    t_d = jnp.concatenate([t_d1, t_d2], axis=1)
    return (
        out,
        grad_in,
        t_q * ga,
        t_k * ga,
        t_v * ga,
        t_o,
        t_g * gf,
        t_u * gf,
        t_d,
        grad_ga,
        grad_gf,
    )


def solution(mesh):
    token = P(("rep", "shard"), None)
    row = P("shard", None)
    return jax.shard_map(
        local,
        mesh=mesh,
        in_specs=(token, P(("rep", "shard")), token) + (row,) * 7 + (P("shard"),) * 2,
        out_specs=(token, token) + (row,) * 7 + (P("shard"),) * 2,
        check_vma=False,
    )
```

```python
import jax
import jax.numpy as jnp
from jax import lax
from jax.sharding import PartitionSpec as P

H = 15
KVH = 5
HD = 64
D = 960
QK = 1280
FF = 2560
EPSILON = 1e-05
THETA = 100000.0
F32 = jnp.float32
BF = jnp.bfloat16
AX = ("rep", "shard")


def device(x, c, z, y):
    return ((x % 4) * 2 + c % 2) * 16 + (z % 4) * 4 + y % 4


def shift(value, axis, step):
    move = {"x": 0, "c": 0, "z": 0, "y": 0, axis: step}
    pairs = [
        (device(x, c, z, y), device(x + move["x"], c + move["c"], z + move["z"], y + move["y"]))
        for x in range(4)
        for c in range(2)
        for z in range(4)
        for y in range(4)
    ]
    return lax.ppermute(value, AX, pairs)


def dot(left, right):
    return jnp.dot(left, right, preferred_element_type=F32)


def dot_t(left, right):
    return lax.dot_general(left, right, (((1,), (1,)), ((), ())), preferred_element_type=F32)


def t_dot(left, right):
    return lax.dot_general(left, right, (((0,), (0,)), ((), ())), preferred_element_type=F32)


def collect(value, axis):
    return [value] + [shift(value, axis, -step) for step in (1, 2, 3)]


def spread(blocks, axis):
    got = [shift(blocks[step], axis, step) for step in (1, 2, 3)]
    total = blocks[0].astype(F32)
    for part in got:
        total = total + part.astype(F32)
    return total.astype(BF)


def gather_rel(value):
    inner = jnp.concatenate(collect(value, "y"), axis=0)
    mine = jnp.concatenate(collect(inner, "z"), axis=0)
    return jnp.concatenate([mine, shift(mine, "c", 1)], axis=0)


def scatter_rel(own, other):
    total = (own + shift(other.astype(BF), "c", 1).astype(F32)).astype(BF)
    for axis in ("z", "y"):
        rows = total.shape[0] // 4
        total = spread([total[i * rows : (i + 1) * rows] for i in range(4)], axis)
    return total


def swap(value):
    return shift(value, "c", 1)


def sum_x(part):
    pair = (part.astype(F32) + shift(part, "x", 2).astype(F32)).astype(BF)
    half = part.shape[0] // 2
    up = shift(pair[:half], "x", 1)
    down = shift(pair[half:], "x", 3)
    other = jnp.concatenate([up, down], axis=0)
    return (pair.astype(F32) + other.astype(F32)).astype(BF)


def by_core(where, mine, other):
    low = where["c"] == 0
    return (jnp.where(low, mine, other), jnp.where(low, other, mine))


def pack_down(value):
    last = value[:, 64:]
    tail = jnp.concatenate([last[:, :, i * 256 : (i + 1) * 256] for i in range(4)], axis=1)
    return jnp.concatenate([value[:, :64], tail], axis=2)


def unpack_down(value):
    tail = value[:, :, 1024:]
    last = jnp.concatenate([tail[:, i * 16 : (i + 1) * 16] for i in range(4)], axis=2)
    return jnp.concatenate([value[:, :, :1024], last], axis=1)


def order_rel(where):
    place = lax.broadcasted_iota(jnp.int32, (D, 1024), 1)
    natural = lax.broadcasted_iota(jnp.int32, (D, 1024), 0)
    core = (where["c"] + place // 512) % 2
    z = (where["z"] + (place // 128) % 4) % 4
    y = (where["y"] + (place // 32) % 4) % 4
    inner = core * 32 + place % 32
    return (((z * 4 + y) * 60 + inner == natural) & (inner < 60)).astype(BF)


def order_abs():
    place = lax.broadcasted_iota(jnp.int32, (D, 1024), 1)
    natural = lax.broadcasted_iota(jnp.int32, (D, 1024), 0)
    inner = place % 64
    return (((place // 64) * 60 + inner == natural) & (inner < 60)).astype(BF)


def rotary_tables(segments):
    count = segments.shape[0]
    index = jnp.arange(count, dtype=jnp.int32)
    same = segments[:, None] == segments[None, :]
    first = jnp.min(jnp.where(same, index[None, :], count), axis=-1)
    position = (index - first).astype(F32)
    half = HD // 2
    freq = THETA ** (-jnp.arange(half, dtype=F32) / half)
    angle = position[:, None] * freq
    return (jnp.cos(angle)[:, None, :], jnp.sin(angle)[:, None, :])


def rotate(values, cos, sin):
    a, b = (values[..., : HD // 2], values[..., HD // 2 :])
    return jnp.concatenate([a * cos - b * sin, b * cos + a * sin], axis=-1)


def unrotate(values, cos, sin):
    a, b = (values[..., : HD // 2], values[..., HD // 2 :])
    return jnp.concatenate([a * cos + b * sin, b * cos - a * sin], axis=-1)


def mult(form, left, right):
    return jnp.einsum(form, left, right, preferred_element_type=F32)


def norm(values):
    scale = lax.rsqrt(jnp.mean(values * values, axis=-1, keepdims=True) + EPSILON)
    return (values * scale, scale)


def norm_back(e, normed, scale):
    return scale * (e - normed * jnp.mean(e * normed, axis=-1, keepdims=True))


def local(x, seg, dy, wq, wk, wv, wo, wg, wu, wd, gain_a, gain_f):
    rep = lax.axis_index("rep")
    shard = lax.axis_index("shard")
    where = {"c": rep % 2, "z": shard // 4, "y": shard % 4}
    core = where["c"]
    ga = gain_a[:, None]
    gf = gain_f[:, None]
    scaled = lambda w, g: (w.astype(F32) * g).astype(BF)
    tall = lambda w: jnp.pad(w, ((0, 4), (0, 0)))
    s_at = jnp.concatenate([scaled(wq, ga), scaled(wk, ga), wo, scaled(wv, ga)], axis=1)
    w_at = gather_rel(lax.dynamic_slice_in_dim(tall(s_at), core * 32, 32, 0))
    w_qk = w_at[:, :QK]
    w_ov = w_at[:, QK:]
    half = lambda w: lax.dynamic_slice_in_dim(w, core * 1280, 1280, 1)
    s_d = jnp.pad(lax.dynamic_slice_in_dim(wd, core * 80, 80, 0), ((0, 0), (0, 64)))
    s_ff = jnp.concatenate(
        [tall(scaled(half(wg), gf)), tall(scaled(half(wu), gf)), pack_down(s_d[None])[0]], axis=1
    )
    w_ff = lax.all_gather(s_ff, "shard", axis=0, tiled=True)
    w_gu = w_ff[:, :FF]
    m_d = unpack_down(w_ff[:, FF:].reshape(16, 64, 1280))
    kept = lax.dynamic_slice_in_dim(m_d, core * 8, 8, 0)
    came = swap(lax.dynamic_slice_in_dim(m_d, (1 - core) * 8, 8, 0))
    w_d = jnp.stack(by_core(where, kept, came), axis=1).reshape(1280, 1024)
    e_rel = order_rel(where)
    e_abs = order_abs()
    dy_wide = jnp.pad(dy, ((0, 0), (0, 64)))
    dy_all = jnp.concatenate([dy_wide, swap(dy_wide)], axis=0)

    xf = x.astype(F32)
    n1, r1 = norm(xf)
    h1 = n1.astype(BF)
    h1p = dot(h1, e_rel).astype(BF)
    cos, sin = rotary_tables(seg)
    qk = dot(h1p, w_qk)
    values = dot(h1p, w_ov)[:, D:].astype(BF).reshape(256, KVH, HD)
    qr = rotate(qk[:, :D].reshape(256, H, HD), cos, sin).astype(BF).reshape(256, KVH, 3, HD)
    kr = rotate(qk[:, D:].reshape(256, KVH, HD), cos, sin).astype(BF)
    index = jnp.arange(256, dtype=jnp.int32)
    allowed = (seg[:, None] == seg[None, :]) & (index[:, None] >= index[None, :])
    allowed = allowed[None, None]
    scores = mult("qkgd,tkd->kgqt", qr, kr) * 0.125
    row_max = jnp.max(jnp.where(allowed, scores, -1e30), axis=-1, keepdims=True)
    weight = jnp.where(allowed, jnp.exp(scores - row_max), 0.0)
    probs = weight / jnp.sum(weight, axis=-1, keepdims=True)
    pb = probs.astype(BF)
    att = mult("kgqt,tkd->qkgd", pb, values).astype(BF).reshape(256, D)
    att_p = dot(att, e_rel).astype(BF)
    w_o = w_ov[:, :D]
    mixed = xf + dot(att_p, w_o)

    n2, r2 = norm(mixed)
    h2p = dot(n2.astype(BF), e_abs).astype(BF)
    h2_all = jnp.concatenate([h2p, swap(h2p)], axis=0)
    gu = dot(h2_all, w_gu)
    gate, up = (gu[:, :1280], gu[:, 1280:])
    sig = jax.nn.sigmoid(gate)
    act = (gate * sig * up).astype(BF)
    y = dot(act, w_d)[:, :D]
    out = (mixed + y[:256] + swap(y[256:].astype(BF)).astype(F32)).astype(BF)

    g_d = t_dot(act, dy_all).astype(BF).reshape(8, 2, 80, 1024)
    kept = lax.dynamic_index_in_dim(g_d, core, 1, keepdims=False)
    came = swap(lax.dynamic_index_in_dim(g_d, 1 - core, 1, keepdims=False))
    g_d = pack_down(jnp.concatenate(by_core(where, kept, came), axis=0)).reshape(1024, 1280)
    d_act = dot_t(dy_all, w_d)
    d_gate = (d_act * up * sig * (1.0 + gate * (1.0 - sig))).astype(BF)
    d_up = (d_act * gate * sig).astype(BF)
    d_gu = jnp.concatenate([d_gate, d_up], axis=1)
    g_ff = jnp.concatenate([t_dot(h2_all, d_gu).astype(BF), g_d], axis=1)
    t_ff = lax.psum_scatter(g_ff, "shard", scatter_dimension=0, tiled=True)
    e_f = dot_t(d_gu, w_gu)
    e_f = (e_f[:256] + swap(e_f[256:].astype(BF)).astype(F32)).astype(BF)
    e_f = dot_t(e_f, e_abs)
    d_mixed = dy.astype(F32) + norm_back(e_f, n2, r2)

    d_attn = d_mixed.astype(BF)
    d_ob = dot_t(dot_t(d_attn, w_o).astype(BF), e_rel).astype(BF).reshape(256, KVH, 3, HD)
    d_vals = mult("kgqt,qkgd->tkd", pb, d_ob)
    d_p = mult("qkgd,tkd->kgqt", d_ob, values)
    row_dot = jnp.sum(probs * d_p, axis=-1, keepdims=True)
    d_s = (probs * (d_p - row_dot) * 0.125).astype(BF)
    d_q = mult("kgqt,tkd->qkgd", d_s, kr).reshape(256, H, HD)
    d_k = mult("kgqt,qkgd->tkd", d_s, qr)
    d_qk = jnp.concatenate(
        [
            unrotate(d_q, cos, sin).astype(BF).reshape(256, D),
            unrotate(d_k, cos, sin).astype(BF).reshape(256, 320),
        ],
        axis=1,
    )
    d_v = d_vals.astype(BF).reshape(256, 320)
    g_at = [
        jnp.concatenate(
            [t_dot(h1p[:, s], d_qk), t_dot(att_p[:, s], d_attn), t_dot(h1p[:, s], d_v)], axis=1
        )
        for s in (slice(0, 512), slice(512, 1024))
    ]
    t_at = sum_x(scatter_rel(g_at[0], g_at[1]))
    t_at = jnp.concatenate(by_core(where, t_at, swap(t_at)), axis=0)[:60].astype(F32)
    d_v_wide = jnp.pad(d_v, ((0, 0), (D, 0)))
    e_a = dot_t(d_qk, w_qk) + dot_t(d_v_wide, w_ov)
    e_a = dot_t(e_a.astype(BF), e_rel)
    grad_in = (d_mixed + norm_back(e_a, n1, r1)).astype(BF)

    t_ff = sum_x(t_ff)
    t_ff = by_core(where, t_ff, swap(t_ff))
    t_g = jnp.concatenate([t[:60, :1280] for t in t_ff], axis=1).astype(F32)
    t_u = jnp.concatenate([t[:60, 1280:FF] for t in t_ff], axis=1).astype(F32)
    t_d = jnp.concatenate([unpack_down(t[None, :, FF:])[0, :, :D] for t in t_ff], axis=0)
    t_q, t_k, t_o, t_v = (t_at[:, :D], t_at[:, D:QK], t_at[:, QK : QK + D], t_at[:, QK + D :])
    rowsum = lambda w, t: jnp.sum(w.astype(F32) * t, axis=1)
    grad_ga = rowsum(wq, t_q) + rowsum(wk, t_k) + rowsum(wv, t_v)
    grad_gf = rowsum(wg, t_g) + rowsum(wu, t_u)
    return (
        out,
        grad_in,
        t_q * ga,
        t_k * ga,
        t_v * ga,
        t_o,
        t_g * gf,
        t_u * gf,
        t_d.astype(F32),
        grad_ga,
        grad_gf,
    )


def solution(mesh):
    token = P(("rep", "shard"), None)
    row = P("shard", None)
    return jax.shard_map(
        local,
        mesh=mesh,
        in_specs=(token, P(("rep", "shard")), token) + (row,) * 7 + (P("shard"),) * 2,
        out_specs=(token, token) + (row,) * 7 + (P("shard"),) * 2,
        check_vma=False,
    )
```

```python
import jax
import jax.numpy as jnp
from jax import lax
from jax.experimental import pallas as pl
from jax.experimental.pallas import tpu as pltpu
from jax.sharding import PartitionSpec as P

H = 15
KVH = 5
HD = 64
D = 960
QK = 1280
FF = 2560
EPSILON = 1e-05
THETA = 100000.0
F32 = jnp.float32
BF = jnp.bfloat16
AX = ("rep", "shard")


def device(x, c, z, y):
    return ((x % 4) * 2 + c % 2) * 16 + (z % 4) * 4 + y % 4


def shift(value, axis, step):
    move = {"x": 0, "c": 0, "z": 0, "y": 0, axis: step}
    pairs = [
        (device(x, c, z, y), device(x + move["x"], c + move["c"], z + move["z"], y + move["y"]))
        for x in range(4)
        for c in range(2)
        for z in range(4)
        for y in range(4)
    ]
    return lax.ppermute(value, AX, pairs)


def dot(left, right):
    return jnp.dot(left, right, preferred_element_type=F32)


def dot_t(left, right):
    return lax.dot_general(left, right, (((1,), (1,)), ((), ())), preferred_element_type=F32)


def t_dot(left, right):
    return lax.dot_general(left, right, (((0,), (0,)), ((), ())), preferred_element_type=F32)


def collect(value, axis):
    return [value] + [shift(value, axis, -step) for step in (1, 2, 3)]


def spread(blocks, axis):
    got = [shift(blocks[step], axis, step) for step in (1, 2, 3)]
    total = blocks[0].astype(F32)
    for part in got:
        total = total + part.astype(F32)
    return total.astype(BF)


def gather_rel(value, where):
    half = lax.dynamic_slice_in_dim(value, where["x"] // 2 * QK, QK, 1)
    inner = jnp.concatenate(collect(half, "y"), axis=0)
    mine = jnp.concatenate(collect(inner, "z"), axis=0)
    parts = by_flag(where["x"] < 2, mine, shift(mine, "x", 2))
    return [jnp.concatenate([part, swap(part)], axis=0) for part in parts]


def scatter_rel(own, other, where):
    total = (own.astype(F32) + swap(other).astype(F32)).astype(BF)
    low = where["x"] < 2
    kept = jnp.where(low, total[:, :QK], total[:, QK:])
    sent = jnp.where(low, total[:, QK:], total[:, :QK])
    total = (kept.astype(F32) + shift(sent, "x", 2).astype(F32)).astype(BF)
    for axis in ("z", "y"):
        rows = total.shape[0] // 4
        total = spread([total[i * rows : (i + 1) * rows] for i in range(4)], axis)
    pairs = [(d, d ^ 32) for d in range(128)]
    total = (total.astype(F32) + lax.ppermute(total, AX, pairs).astype(F32)).astype(BF)
    return jnp.concatenate(by_flag(low, total, shift(total, "x", 2)), axis=1)


def swap(value):
    return shift(value, "c", 1)


def sum_x(part, where):
    blocks = part.reshape(4, 16, part.shape[1])
    at = [(where["x"] + step) % 4 for step in range(4)]
    total = spread(
        [lax.dynamic_index_in_dim(blocks, at[step], 0, keepdims=False) for step in range(4)], "x"
    )
    whole = jnp.zeros_like(blocks)
    for step, got in enumerate(collect(total, "x")):
        whole = lax.dynamic_update_slice(whole, got[None], (at[step], 0, 0))
    return whole.reshape(part.shape)


def by_flag(low, mine, other):
    return (jnp.where(low, mine, other), jnp.where(low, other, mine))


def pack_down(value):
    last = value[:, 64:]
    tail = jnp.concatenate([last[:, :, i * 256 : (i + 1) * 256] for i in range(4)], axis=1)
    return jnp.concatenate([value[:, :64], tail], axis=2)


def unpack_down(value):
    tail = value[:, :, 1024:]
    last = jnp.concatenate([tail[:, i * 16 : (i + 1) * 16] for i in range(4)], axis=2)
    return jnp.concatenate([value[:, :, :1024], last], axis=1)


def order_rel(where):
    place = lax.broadcasted_iota(jnp.int32, (D, 1024), 1)
    natural = lax.broadcasted_iota(jnp.int32, (D, 1024), 0)
    core = (where["c"] + place // 512) % 2
    z = (where["z"] + (place // 128) % 4) % 4
    y = (where["y"] + (place // 32) % 4) % 4
    inner = core * 32 + place % 32
    return (((z * 4 + y) * 60 + inner == natural) & (inner < 60)).astype(BF)


def order_abs():
    place = lax.broadcasted_iota(jnp.int32, (D, 1024), 1)
    natural = lax.broadcasted_iota(jnp.int32, (D, 1024), 0)
    inner = place % 64
    return (((place // 64) * 60 + inner == natural) & (inner < 60)).astype(BF)


def rotary_tables(segments):
    count = segments.shape[0]
    index = jnp.arange(count, dtype=jnp.int32)
    same = segments[:, None] == segments[None, :]
    first = jnp.min(jnp.where(same, index[None, :], count), axis=-1)
    position = (index - first).astype(F32)
    half = HD // 2
    freq = THETA ** (-jnp.arange(half, dtype=F32) / half)
    angle = position[:, None] * freq
    cos, sin = (jnp.cos(angle), jnp.sin(angle))
    return (
        jnp.concatenate([cos] * 4, axis=1),
        jnp.concatenate([-sin, sin, -sin, sin], axis=1),
    )


def norm(values):
    scale = lax.rsqrt(jnp.mean(values * values, axis=-1, keepdims=True) + EPSILON)
    return (values * scale, scale)


def norm_back(e, normed, scale):
    return scale * (e - normed * jnp.mean(e * normed, axis=-1, keepdims=True))


def swap_halves(block):
    lane = lax.broadcasted_iota(jnp.int32, block.shape, 1)
    return jnp.where(lane % 64 < 32, pltpu.roll(block, 96, 1), pltpu.roll(block, 32, 1))


def forward_kernel(
    x_ref, h1p_ref, wqk_ref, wov_ref, erel_ref, eabs_ref, cos_ref, sin_ref, segc_ref, segr_ref,
    qkr_ref, v_ref, pb_ref, attp_ref, mixed_ref, h2p_ref, att_ref,
):
    h1p = h1p_ref[...]
    cos, sin = (cos_ref[...], sin_ref[...])
    for i in range(10):
        lanes = slice(128 * i, 128 * i + 128)
        part = dot(h1p, wqk_ref[:, lanes])
        qkr_ref[:, lanes] = (part * cos + swap_halves(part) * sin).astype(BF)
    v_ref[...] = dot(h1p, wov_ref[:, 896:1280]).astype(BF)
    row = lax.broadcasted_iota(jnp.int32, (256, 256), 0)
    col = lax.broadcasted_iota(jnp.int32, (256, 256), 1)
    allowed = (segc_ref[...] == segr_ref[...]) & (row >= col)
    for h in range(H):
        g = h // 3
        q = qkr_ref[:, 64 * h : 64 * h + 64]
        k = qkr_ref[:, D + 64 * g : D + 64 * g + 64]
        scores = jnp.where(allowed, dot_t(q, k) * 0.125, -1e30)
        weight = jnp.exp(scores - jnp.max(scores, axis=-1, keepdims=True))
        pb = (weight / jnp.sum(weight, axis=-1, keepdims=True)).astype(BF)
        pb_ref[h] = pb
        att_ref[:, 64 * h : 64 * h + 64] = dot(pb, v_ref[:, 64 + 64 * g : 128 + 64 * g]).astype(BF)
    att_p = dot(att_ref[...], erel_ref[...]).astype(BF)
    attp_ref[...] = att_p
    mixed = x_ref[...].astype(F32) + dot(att_p, wov_ref[:, :D])
    mixed_ref[...] = mixed
    h2p_ref[...] = dot(norm(mixed)[0].astype(BF), eabs_ref[...]).astype(BF)


def ffn_kernel(h2_ref, dy_ref, wg_ref, wu_ref, wd_ref, gg_ref, gd_ref, y_ref, ef_ref, h2t_ref):
    @pl.when(pl.program_id(0) == 0)
    def _():
        h2t_ref[...] = h2_ref[...].T
        y_ref[...] = jnp.zeros_like(y_ref)
        ef_ref[...] = jnp.zeros_like(ef_ref)

    h2, dy, wg, wu, wd = (h2_ref[...], dy_ref[...], wg_ref[...], wu_ref[...], wd_ref[...])
    gate, up, d_act = (dot(h2, wg), dot(h2, wu), dot_t(dy, wd))
    sig = jax.nn.sigmoid(gate)
    silu = gate * sig
    act = (silu * up).astype(BF)
    d_gate = (d_act * up * sig * (1.0 + gate * (1.0 - sig))).astype(BF)
    d_up = (d_act * silu).astype(BF)
    gg_ref[:, :256] = dot(h2t_ref[...], d_gate).astype(BF)
    gg_ref[:, 256:] = dot(h2t_ref[...], d_up).astype(BF)
    gd_ref[...] = dot(act.T, dy).astype(BF)
    y_ref[...] += dot(act, wd)
    ef_ref[...] += dot_t(d_gate, wg) + dot_t(d_up, wu)


def backward_kernel(
    ef_ref, came_ref, dy_ref, mixed_ref, h1p_ref, attp_ref, qkr_ref, v_ref, pb_ref, wov_ref,
    erel_ref, eabs_ref, cos_ref, sin_ref,
    dmixed_ref, dqk_ref, dv_ref, own_ref, other_ref, dob_ref, raw_ref, da_ref,
):
    e = dot_t((ef_ref[...] + came_ref[...].astype(F32)).astype(BF), eabs_ref[...])
    n2, r2 = norm(mixed_ref[...])
    d_mixed = dy_ref[...].astype(F32) + norm_back(e, n2, r2)
    dmixed_ref[...] = d_mixed
    d_attn = d_mixed.astype(BF)
    da_ref[:, :D] = d_attn
    da_ref[:, D:] = jnp.zeros((256, 320), BF)
    d_ob_p = dot_t(d_attn, wov_ref[:, :D]).astype(BF)
    dob_ref[...] = dot_t(d_ob_p, erel_ref[...]).astype(BF)
    dv_ref[:, :D] = jnp.zeros((256, D), BF)
    for g in range(KVH):
        k = qkr_ref[:, D + 64 * g : D + 64 * g + 64]
        v = v_ref[:, 64 + 64 * g : 128 + 64 * g]
        d_v = jnp.zeros((256, HD), F32)
        d_k = jnp.zeros((256, HD), F32)
        for h in range(3 * g, 3 * g + 3):
            pb = pb_ref[h]
            d_ob = dob_ref[:, 64 * h : 64 * h + 64]
            d_p = dot_t(d_ob, v)
            probs = pb.astype(F32)
            row_dot = jnp.sum(probs * d_p, axis=-1, keepdims=True)
            d_s = (probs * (d_p - row_dot) * 0.125).astype(BF)
            raw_ref[:, 64 * h : 64 * h + 64] = dot(d_s, k)
            d_v += t_dot(pb, d_ob)
            d_k += t_dot(d_s, qkr_ref[:, 64 * h : 64 * h + 64])
        raw_ref[:, D + 64 * g : D + 64 * g + 64] = d_k
        dv_ref[:, D + 64 * g : D + 64 * g + 64] = d_v.astype(BF)
    cos, sin = (cos_ref[...], sin_ref[...])
    for i in range(10):
        lanes = slice(128 * i, 128 * i + 128)
        part = raw_ref[:, lanes]
        dqk_ref[:, lanes] = (part * cos - swap_halves(part) * sin).astype(BF)
    for ref, rows in ((other_ref, slice(512, 1024)), (own_ref, slice(0, 512))):
        h1t = h1p_ref[:, rows].T
        att = attp_ref[:, rows].T
        ref[:, :QK] = dot(h1t, dqk_ref[...]).astype(BF)
        ref[:, QK:] = (dot(att, da_ref[...]) + dot(h1t, dv_ref[...])).astype(BF)


def kernel_call(kernel, outs, scratch, flops, *args):
    whole = pl.BlockSpec(memory_space=pltpu.VMEM)
    shapes = [jax.ShapeDtypeStruct(*out) for out in outs]
    size = sum(s.size * s.dtype.itemsize for s in list(args) + shapes)
    return pl.pallas_call(
        kernel,
        out_shape=shapes,
        in_specs=[whole] * len(args),
        out_specs=[whole] * len(outs),
        scratch_shapes=[pltpu.VMEM(*s) for s in scratch],
        compiler_params=pltpu.CompilerParams(vmem_limit_bytes=44 * 2**20),
        cost_estimate=pl.CostEstimate(flops=flops, bytes_accessed=size, transcendentals=0),
    )(*args)


def ffn_call(h2, dy, w_ff, w_d):
    fixed = lambda j: (0, 0)
    return pl.pallas_call(
        ffn_kernel,
        grid=(5,),
        out_shape=[
            jax.ShapeDtypeStruct((1024, 3840), BF),
            jax.ShapeDtypeStruct((1280, 1024), BF),
            jax.ShapeDtypeStruct((512, 1024), F32),
            jax.ShapeDtypeStruct((512, 1024), F32),
        ],
        in_specs=[
            pl.BlockSpec((512, 1024), fixed),
            pl.BlockSpec((512, 1024), fixed),
            pl.BlockSpec((1024, 256), lambda j: (0, j)),
            pl.BlockSpec((1024, 256), lambda j: (0, 5 + j)),
            pl.BlockSpec((256, 1024), lambda j: (j, 0)),
        ],
        out_specs=[
            pl.BlockSpec((1024, 512), lambda j: (0, j)),
            pl.BlockSpec((256, 1024), lambda j: (j, 0)),
            pl.BlockSpec((512, 1024), fixed),
            pl.BlockSpec((512, 1024), fixed),
        ],
        scratch_shapes=[pltpu.VMEM((1024, 512), BF)],
        compiler_params=pltpu.CompilerParams(vmem_limit_bytes=44 * 2**20),
        cost_estimate=pl.CostEstimate(
            flops=12 * 10**9, bytes_accessed=32 * 10**6, transcendentals=512 * 1280
        ),
    )(h2, dy, w_ff, w_ff, w_d)


def local(x, seg, dy, wq, wk, wv, wo, wg, wu, wd, gain_a, gain_f):
    rep = lax.axis_index("rep")
    shard = lax.axis_index("shard")
    where = {"x": rep // 2, "c": rep % 2, "z": shard // 4, "y": shard % 4}
    core = where["c"]
    ga = gain_a[:, None]
    gf = gain_f[:, None]
    scaled = lambda w, g: (w.astype(F32) * g).astype(BF)
    tall = lambda w: jnp.pad(w, ((0, 4), (0, 0)))
    s_at = jnp.concatenate([scaled(wq, ga), scaled(wk, ga), wo, scaled(wv, ga)], axis=1)
    w_qk, w_ov = gather_rel(lax.dynamic_slice_in_dim(tall(s_at), core * 32, 32, 0), where)
    half = lambda w: lax.dynamic_slice_in_dim(w, core * 1280, 1280, 1)
    s_d = jnp.pad(lax.dynamic_slice_in_dim(wd, core * 80, 80, 0), ((0, 0), (0, 64)))
    s_ff = jnp.concatenate(
        [tall(scaled(half(wg), gf)), tall(scaled(half(wu), gf)), pack_down(s_d[None])[0]], axis=1
    )
    w_ff = lax.all_gather(s_ff, "shard", axis=0, tiled=True)
    m_d = unpack_down(w_ff[:, FF:].reshape(16, 64, 1280))
    kept = lax.dynamic_slice_in_dim(m_d, core * 8, 8, 0)
    came = swap(lax.dynamic_slice_in_dim(m_d, (1 - core) * 8, 8, 0))
    w_d = jnp.stack(by_flag(core == 0, kept, came), axis=1).reshape(1280, 1024)
    e_rel = order_rel(where)
    e_abs = order_abs()
    dy_wide = jnp.pad(dy, ((0, 0), (0, 64)))
    dy_all = jnp.concatenate([dy_wide, swap(dy_wide)], axis=0)

    n1, r1 = norm(x.astype(F32))
    h1p = dot(n1.astype(BF), e_rel).astype(BF)
    cos, sin = rotary_tables(seg)
    qkr, values, pb, att_p, mixed, h2p = kernel_call(
        forward_kernel,
        [((256, QK), BF), ((256, 384), BF), ((H, 256, 256), BF), ((256, 1024), BF),
         ((256, D), F32), ((256, 1024), BF)],
        [((256, D), BF)],
        4 * 10**9,
        x, h1p, w_qk, w_ov, e_rel, e_abs, cos, sin, seg[:, None], seg[None, :],
    )

    h2_all = jnp.concatenate([h2p, swap(h2p)], axis=0)
    g_ff, g_d, y, e_f = ffn_call(h2_all, dy_all, w_ff, w_d)
    g_d = g_d.reshape(8, 2, 80, 1024)
    kept = lax.dynamic_index_in_dim(g_d, core, 1, keepdims=False)
    came = swap(lax.dynamic_index_in_dim(g_d, 1 - core, 1, keepdims=False))
    g_d = pack_down(jnp.concatenate(by_flag(core == 0, kept, came), axis=0)).reshape(1024, 1280)
    g_ff = lax.dynamic_update_slice(g_ff, g_d, (0, FF))
    t_ff = lax.psum_scatter(g_ff, "shard", scatter_dimension=0, tiled=True)
    out = (mixed + y[:256, :D] + swap(y[256:].astype(BF)).astype(F32)[:, :D]).astype(BF)

    d_mixed, d_qk, d_v, g_own, g_other = kernel_call(
        backward_kernel,
        [((256, D), F32), ((256, QK), BF), ((256, QK), BF), ((512, FF), BF), ((512, FF), BF)],
        [((256, D), BF), ((256, QK), F32), ((256, QK), BF)],
        6 * 10**9,
        e_f[:256], swap(e_f[256:].astype(BF)), dy, mixed, h1p, att_p, qkr, values, pb, w_ov,
        e_rel, e_abs, cos, sin,
    )
    t_at = scatter_rel(g_own, g_other, where)
    t_at = jnp.concatenate(by_flag(core == 0, t_at, swap(t_at)), axis=0)[:60].astype(F32)
    e_a = dot_t(d_qk, w_qk) + dot_t(d_v, w_ov)
    e_a = dot_t(e_a.astype(BF), e_rel)
    grad_in = (d_mixed + norm_back(e_a, n1, r1)).astype(BF)

    t_ff = sum_x(t_ff, where)
    t_ff = by_flag(core == 0, t_ff, swap(t_ff))
    columns = lambda at: jnp.concatenate(
        [t[:60, at + 512 * j : at + 512 * j + 256] for t in t_ff for j in range(5)], axis=1
    ).astype(F32)
    t_g, t_u = (columns(0), columns(256))
    t_d = jnp.concatenate([unpack_down(t[None, :, FF:])[0, :, :D] for t in t_ff], axis=0)
    t_q, t_k, t_o, t_v = (t_at[:, :D], t_at[:, D:QK], t_at[:, QK : QK + D], t_at[:, QK + D :])
    rowsum = lambda w, t: jnp.sum(w.astype(F32) * t, axis=1)
    grad_ga = rowsum(wq, t_q) + rowsum(wk, t_k) + rowsum(wv, t_v)
    grad_gf = rowsum(wg, t_g) + rowsum(wu, t_u)
    return (
        out,
        grad_in,
        t_q * ga,
        t_k * ga,
        t_v * ga,
        t_o,
        t_g * gf,
        t_u * gf,
        t_d.astype(F32),
        grad_ga,
        grad_gf,
    )


def solution(mesh):
    token = P(("rep", "shard"), None)
    row = P("shard", None)
    return jax.shard_map(
        local,
        mesh=mesh,
        in_specs=(token, P(("rep", "shard")), token) + (row,) * 7 + (P("shard"),) * 2,
        out_specs=(token, token) + (row,) * 7 + (P("shard"),) * 2,
        check_vma=False,
    )
```

```python
import jax
import jax.numpy as jnp
from jax import lax
from jax.experimental import pallas as pl
from jax.experimental.pallas import tpu as pltpu
from jax.sharding import PartitionSpec as P

H = 15
KVH = 5
HD = 64
D = 960
QK = 1280
FF = 2560
EPSILON = 1e-05
THETA = 100000.0
F32 = jnp.float32
BF = jnp.bfloat16
AX = ("rep", "shard")


def device(x, c, z, y):
    return ((x % 4) * 2 + c % 2) * 16 + (z % 4) * 4 + y % 4


def shift(value, axis, step):
    move = {"x": 0, "c": 0, "z": 0, "y": 0, axis: step}
    pairs = [
        (device(x, c, z, y), device(x + move["x"], c + move["c"], z + move["z"], y + move["y"]))
        for x in range(4)
        for c in range(2)
        for z in range(4)
        for y in range(4)
    ]
    return lax.ppermute(value, AX, pairs)


def dot(left, right):
    return jnp.dot(left, right, preferred_element_type=F32)


def dot_t(left, right):
    return lax.dot_general(left, right, (((1,), (1,)), ((), ())), preferred_element_type=F32)


def t_dot(left, right):
    return lax.dot_general(left, right, (((0,), (0,)), ((), ())), preferred_element_type=F32)


def collect(value, axis):
    return [value] + [shift(value, axis, -step) for step in (1, 2, 3)]


def spread(blocks, axis):
    got = [shift(blocks[step], axis, step) for step in (1, 2, 3)]
    total = blocks[0].astype(F32)
    for part in got:
        total = total + part.astype(F32)
    return total.astype(BF)


def gather_rel(value, first, second):
    inner = jnp.concatenate(collect(value, first), axis=0)
    mine = jnp.concatenate(collect(inner, second), axis=0)
    return [mine, swap(mine)]


def scatter_rel(own, other, first, second):
    total = (own.astype(F32) + swap(other).astype(F32)).astype(BF)
    for axis in (first, second):
        rows = total.shape[0] // 4
        total = spread([total[i * rows : (i + 1) * rows] for i in range(4)], axis)
    return total


def all_x(part):
    one, two, three = [shift(part, "x", step) for step in (1, 2, 3)]
    total = (part.astype(F32) + two.astype(F32)) + (one.astype(F32) + three.astype(F32))
    return total.astype(BF)


def swap(value):
    return shift(value, "c", 1)


def sum_x(part, where):
    blocks = part.reshape(4, 16, part.shape[1])
    at = [(where["x"] + step) % 4 for step in range(4)]
    total = spread(
        [lax.dynamic_index_in_dim(blocks, at[step], 0, keepdims=False) for step in range(4)], "x"
    )
    whole = jnp.zeros_like(blocks)
    for step, got in enumerate(collect(total, "x")):
        whole = lax.dynamic_update_slice(whole, got[None], (at[step], 0, 0))
    return whole.reshape(part.shape)


def by_flag(low, mine, other):
    return (jnp.where(low, mine, other), jnp.where(low, other, mine))


def pack_down(value):
    last = value[:, 64:]
    tail = jnp.concatenate([last[:, :, i * 256 : (i + 1) * 256] for i in range(4)], axis=1)
    return jnp.concatenate([value[:, :64], tail], axis=2)


def unpack_down(value):
    tail = value[:, :, 1024:]
    last = jnp.concatenate([tail[:, i * 16 : (i + 1) * 16] for i in range(4)], axis=2)
    return jnp.concatenate([value[:, :, :1024], last], axis=1)


def order_rel(where, major, minor):
    place = lax.broadcasted_iota(jnp.int32, (D, 1024), 1)
    natural = lax.broadcasted_iota(jnp.int32, (D, 1024), 0)
    core = (where["c"] + place // 512) % 2
    at = {
        major: (where[major] + (place // 128) % 4) % 4,
        minor: (where[minor] + (place // 32) % 4) % 4,
    }
    inner = core * 32 + place % 32
    return (((at["z"] * 4 + at["y"]) * 60 + inner == natural) & (inner < 60)).astype(BF)


def order_abs():
    place = lax.broadcasted_iota(jnp.int32, (D, 1024), 1)
    natural = lax.broadcasted_iota(jnp.int32, (D, 1024), 0)
    inner = place % 64
    return (((place // 64) * 60 + inner == natural) & (inner < 60)).astype(BF)


def rotary_tables(segments):
    count = segments.shape[0]
    index = jnp.arange(count, dtype=jnp.int32)
    same = segments[:, None] == segments[None, :]
    first = jnp.min(jnp.where(same, index[None, :], count), axis=-1)
    position = (index - first).astype(F32)
    half = HD // 2
    freq = THETA ** (-jnp.arange(half, dtype=F32) / half)
    angle = position[:, None] * freq
    cos, sin = (jnp.cos(angle), jnp.sin(angle))
    return (
        jnp.concatenate([cos] * 4, axis=1),
        jnp.concatenate([-sin, sin, -sin, sin], axis=1),
    )


def norm(values):
    scale = lax.rsqrt(jnp.mean(values * values, axis=-1, keepdims=True) + EPSILON)
    return (values * scale, scale)


def norm_back(e, normed, scale):
    return scale * (e - normed * jnp.mean(e * normed, axis=-1, keepdims=True))


def swap_halves(block):
    lane = lax.broadcasted_iota(jnp.int32, block.shape, 1)
    return jnp.where(lane % 64 < 32, pltpu.roll(block, 96, 1), pltpu.roll(block, 32, 1))


def forward_kernel(
    x_ref, h1a_ref, h1b_ref, wqk_ref, wqk2_ref, wov_ref, wov2_ref, erel_ref, eabs_ref,
    cos_ref, sin_ref, segc_ref, segr_ref,
    qkr_ref, v_ref, pb_ref, attp_ref, mixed_ref, h2p_ref, att_ref,
):
    cos, sin = (cos_ref[...], sin_ref[...])
    for i in range(10):
        lanes = slice(128 * i, 128 * i + 128)
        part = dot(h1a_ref[:, :512], wqk_ref[:, lanes]) + dot(h1a_ref[:, 512:], wqk2_ref[:, lanes])
        qkr_ref[:, lanes] = (part * cos + swap_halves(part) * sin).astype(BF)
    v_ref[...] = (
        dot(h1b_ref[:, :512], wov_ref[:, 896:1280]) + dot(h1b_ref[:, 512:], wov2_ref[:, 896:1280])
    ).astype(BF)
    row = lax.broadcasted_iota(jnp.int32, (256, 256), 0)
    col = lax.broadcasted_iota(jnp.int32, (256, 256), 1)
    allowed = (segc_ref[...] == segr_ref[...]) & (row >= col)
    for h in range(H):
        g = h // 3
        q = qkr_ref[:, 64 * h : 64 * h + 64]
        k = qkr_ref[:, D + 64 * g : D + 64 * g + 64]
        scores = jnp.where(allowed, dot_t(q, k) * 0.125, -1e30)
        weight = jnp.exp(scores - jnp.max(scores, axis=-1, keepdims=True))
        pb = (weight / jnp.sum(weight, axis=-1, keepdims=True)).astype(BF)
        pb_ref[h] = pb
        att_ref[:, 64 * h : 64 * h + 64] = dot(pb, v_ref[:, 64 + 64 * g : 128 + 64 * g]).astype(BF)
    att_p = dot(att_ref[...], erel_ref[...]).astype(BF)
    attp_ref[...] = att_p
    mixed = (
        x_ref[...].astype(F32)
        + dot(att_p[:, :512], wov_ref[:, :D])
        + dot(att_p[:, 512:], wov2_ref[:, :D])
    )
    mixed_ref[...] = mixed
    h2p_ref[...] = dot(norm(mixed)[0].astype(BF), eabs_ref[...]).astype(BF)


def ffn_kernel(
    h2a_ref, h2b_ref, dya_ref, dyb_ref, wg_ref, wu_ref, wd_ref,
    dgu_ref, gd_ref, ya_ref, yb_ref, h2t_ref, h2_ref, dy_ref,
):
    @pl.when(pl.program_id(0) == 0)
    def _():
        h2_ref[:256] = h2a_ref[...]
        h2_ref[256:] = h2b_ref[...]
        dy_ref[:256] = dya_ref[...]
        dy_ref[256:] = dyb_ref[...]
        h2t_ref[...] = h2_ref[...].T
        ya_ref[...] = jnp.zeros_like(ya_ref)
        yb_ref[...] = jnp.zeros_like(yb_ref)

    h2, dy, wd = (h2_ref[...], dy_ref[...], wd_ref[...])
    gate, up, d_act = (dot(h2, wg_ref[...]), dot(h2, wu_ref[...]), dot_t(dy, wd))
    sig = jax.nn.sigmoid(gate)
    silu = gate * sig
    act = (silu * up).astype(BF)
    dgu_ref[:, :256] = (d_act * up * sig * (1.0 + gate * (1.0 - sig))).astype(BF)
    dgu_ref[:, 256:] = (d_act * silu).astype(BF)
    gd_ref[...] = dot(act.T, dy).astype(BF)
    ya_ref[...] += dot(act[:256], wd)
    yb_ref[...] += dot(act[256:], wd)


def ffn_grad_kernel(h2t_ref, dgu_ref, wg_ref, wu_ref, gg_ref, ea_ref, eb_ref, total_ref):
    j = pl.program_id(0)

    @pl.when(j == 0)
    def _():
        total_ref[...] = jnp.zeros_like(total_ref)

    dgu = dgu_ref[...]
    gg_ref[...] = dot(h2t_ref[...], dgu).astype(BF)
    total_ref[...] += dot_t(dgu[:, :256], wg_ref[...]) + dot_t(dgu[:, 256:], wu_ref[...])

    @pl.when(j == 4)
    def _():
        ea_ref[...] = total_ref[:256]
        eb_ref[...] = total_ref[256:].astype(BF)


def backward_kernel(
    ef_ref, came_ref, dy_ref, mixed_ref, h1a_ref, h1b_ref, attp_ref, qkr_ref, v_ref, pb_ref,
    wqk_ref, wqk2_ref, wov_ref, wov2_ref, ea_ref, erel_ref, eabs_ref, cos_ref, sin_ref, x_ref,
    gin_ref, qk_own_ref, ov_own_ref, qk_other_ref, ov_other_ref,
    dob_ref, raw_ref, da_ref, dqk_ref, dv_ref, dmixed_ref,
):
    e = dot_t((ef_ref[...] + came_ref[...].astype(F32)).astype(BF), eabs_ref[...])
    n2, r2 = norm(mixed_ref[...])
    d_mixed = dy_ref[...].astype(F32) + norm_back(e, n2, r2)
    dmixed_ref[...] = d_mixed
    d_attn = d_mixed.astype(BF)
    da_ref[:, :D] = d_attn
    da_ref[:, D:] = jnp.zeros((256, 320), BF)
    dob_ref[...] = (
        dot_t(dot_t(d_attn, wov_ref[:, :D]).astype(BF), erel_ref[:, :512])
        + dot_t(dot_t(d_attn, wov2_ref[:, :D]).astype(BF), erel_ref[:, 512:])
    ).astype(BF)
    dv_ref[:, :D] = jnp.zeros((256, D), BF)
    for g in range(KVH):
        k = qkr_ref[:, D + 64 * g : D + 64 * g + 64]
        v = v_ref[:, 64 + 64 * g : 128 + 64 * g]
        d_v = jnp.zeros((256, HD), F32)
        d_k = jnp.zeros((256, HD), F32)
        for h in range(3 * g, 3 * g + 3):
            pb = pb_ref[h]
            d_ob = dob_ref[:, 64 * h : 64 * h + 64]
            d_p = dot_t(d_ob, v)
            probs = pb.astype(F32)
            row_dot = jnp.sum(probs * d_p, axis=-1, keepdims=True)
            d_s = (probs * (d_p - row_dot) * 0.125).astype(BF)
            raw_ref[:, 64 * h : 64 * h + 64] = dot(d_s, k)
            d_v += t_dot(pb, d_ob)
            d_k += t_dot(d_s, qkr_ref[:, 64 * h : 64 * h + 64])
        raw_ref[:, D + 64 * g : D + 64 * g + 64] = d_k
        dv_ref[:, D + 64 * g : D + 64 * g + 64] = d_v.astype(BF)
    cos, sin = (cos_ref[...], sin_ref[...])
    for i in range(10):
        lanes = slice(128 * i, 128 * i + 128)
        part = raw_ref[:, lanes]
        dqk_ref[:, lanes] = (part * cos - swap_halves(part) * sin).astype(BF)
    for qk_ref, ov_ref, rows in (
        (qk_other_ref, ov_other_ref, slice(512, 1024)),
        (qk_own_ref, ov_own_ref, slice(0, 512)),
    ):
        qk_ref[...] = dot(h1a_ref[:, rows].T, dqk_ref[...]).astype(BF)
        ov_ref[...] = (
            dot(attp_ref[:, rows].T, da_ref[...]) + dot(h1b_ref[:, rows].T, dv_ref[...])
        ).astype(BF)
    e = (
        dot_t(dot_t(dqk_ref[...], wqk_ref[...]).astype(BF), ea_ref[:, :512])
        + dot_t(dot_t(dqk_ref[...], wqk2_ref[...]).astype(BF), ea_ref[:, 512:])
        + dot_t(dot_t(dv_ref[:, 896:], wov_ref[:, 896:]).astype(BF), erel_ref[:, :512])
        + dot_t(dot_t(dv_ref[:, 896:], wov2_ref[:, 896:]).astype(BF), erel_ref[:, 512:])
    )
    n1, r1 = norm(x_ref[...].astype(F32))
    gin_ref[...] = (dmixed_ref[...] + norm_back(e, n1, r1)).astype(BF)


def kernel_call(kernel, outs, scratch, mib, flops, *args):
    whole = pl.BlockSpec(memory_space=pltpu.VMEM)
    shapes = [jax.ShapeDtypeStruct(*out) for out in outs]
    size = sum(s.size * s.dtype.itemsize for s in list(args) + shapes)
    return pl.pallas_call(
        kernel,
        out_shape=shapes,
        in_specs=[whole] * len(args),
        out_specs=[whole] * len(outs),
        scratch_shapes=[pltpu.VMEM(*s) for s in scratch],
        compiler_params=pltpu.CompilerParams(vmem_limit_bytes=mib * 2**20),
        cost_estimate=pl.CostEstimate(flops=flops, bytes_accessed=size, transcendentals=0),
    )(*args)


def ffn_call(h2a, h2b, dya, dyb, w_ff, w_d):
    fixed = lambda j: (0, 0)
    token = pl.BlockSpec((256, 1024), fixed)
    return pl.pallas_call(
        ffn_kernel,
        grid=(5,),
        out_shape=[
            jax.ShapeDtypeStruct((512, 2560), BF),
            jax.ShapeDtypeStruct((1280, 1024), BF),
            jax.ShapeDtypeStruct((256, 1024), F32),
            jax.ShapeDtypeStruct((256, 1024), F32),
            jax.ShapeDtypeStruct((1024, 512), BF),
        ],
        in_specs=[token] * 4
        + [
            pl.BlockSpec((1024, 256), lambda j: (0, j)),
            pl.BlockSpec((1024, 256), lambda j: (0, 5 + j)),
            pl.BlockSpec((256, 1024), lambda j: (j, 0)),
        ],
        out_specs=[
            pl.BlockSpec((512, 512), lambda j: (0, j)),
            pl.BlockSpec((256, 1024), lambda j: (j, 0)),
            token,
            token,
            pl.BlockSpec((1024, 512), fixed),
        ],
        scratch_shapes=[pltpu.VMEM((512, 1024), BF), pltpu.VMEM((512, 1024), BF)],
        compiler_params=pltpu.CompilerParams(vmem_limit_bytes=22 * 2**20),
        cost_estimate=pl.CostEstimate(
            flops=7 * 10**9, bytes_accessed=20 * 10**6, transcendentals=512 * 1280
        ),
    )(h2a, h2b, dya, dyb, w_ff, w_ff, w_d)


def ffn_grad_call(h2t, dgu, w_ff):
    fixed = lambda j: (0, 0)
    token = pl.BlockSpec((256, 1024), fixed)
    return pl.pallas_call(
        ffn_grad_kernel,
        grid=(5,),
        out_shape=[
            jax.ShapeDtypeStruct((1024, 3840), BF),
            jax.ShapeDtypeStruct((256, 1024), F32),
            jax.ShapeDtypeStruct((256, 1024), BF),
        ],
        in_specs=[
            pl.BlockSpec((1024, 512), fixed),
            pl.BlockSpec((512, 512), lambda j: (0, j)),
            pl.BlockSpec((1024, 256), lambda j: (0, j)),
            pl.BlockSpec((1024, 256), lambda j: (0, 5 + j)),
        ],
        out_specs=[pl.BlockSpec((1024, 512), lambda j: (0, j)), token, token],
        scratch_shapes=[pltpu.VMEM((512, 1024), F32)],
        compiler_params=pltpu.CompilerParams(vmem_limit_bytes=18 * 2**20),
        cost_estimate=pl.CostEstimate(
            flops=6 * 10**9, bytes_accessed=16 * 10**6, transcendentals=0
        ),
    )(h2t, dgu, w_ff, w_ff)


def local(x, seg, dy, wq, wk, wv, wo, wg, wu, wd, gain_a, gain_f):
    rep = lax.axis_index("rep")
    shard = lax.axis_index("shard")
    where = {"x": rep // 2, "c": rep % 2, "z": shard // 4, "y": shard % 4}
    core = where["c"]
    ga = gain_a[:, None]
    gf = gain_f[:, None]
    scaled = lambda w, g: (w.astype(F32) * g).astype(BF)
    tall = lambda w: jnp.pad(w, ((0, 4), (0, 0)))
    mine = lambda *w: lax.dynamic_slice_in_dim(tall(jnp.concatenate(w, axis=1)), core * 32, 32, 0)
    w_qk = gather_rel(mine(scaled(wq, ga), scaled(wk, ga)), "y", "z")
    w_ov = gather_rel(mine(wo, scaled(wv, ga)), "z", "y")
    half = lambda w: lax.dynamic_slice_in_dim(w, core * 1280, 1280, 1)
    s_d = jnp.pad(lax.dynamic_slice_in_dim(wd, core * 80, 80, 0), ((0, 0), (0, 64)))
    s_ff = jnp.concatenate(
        [tall(scaled(half(wg), gf)), tall(scaled(half(wu), gf)), pack_down(s_d[None])[0]], axis=1
    )
    w_ff = lax.all_gather(s_ff, "shard", axis=0, tiled=True)
    e_a = order_rel(where, "z", "y")
    e_b = order_rel(where, "y", "z")
    e_abs = order_abs()
    dy_wide = jnp.pad(dy, ((0, 0), (0, 64)))
    dy_other = swap(dy_wide)

    n1, r1 = norm(x.astype(F32))
    h1 = n1.astype(BF)
    h1a = dot(h1, e_a).astype(BF)
    h1b = dot(h1, e_b).astype(BF)
    cos, sin = rotary_tables(seg)
    qkr, values, pb, att_p, mixed, h2p = kernel_call(
        forward_kernel,
        [((256, QK), BF), ((256, 384), BF), ((H, 256, 256), BF), ((256, 1024), BF),
         ((256, D), F32), ((256, 1024), BF)],
        [((256, D), BF)],
        12,
        4 * 10**9,
        x, h1a, h1b, *w_qk, *w_ov, e_b, e_abs, cos, sin, seg[:, None], seg[None, :],
    )

    w_ff, h2p = lax.optimization_barrier((w_ff, h2p))
    m_d = unpack_down(w_ff[:, FF:].reshape(16, 64, 1280))
    kept = lax.dynamic_slice_in_dim(m_d, core * 8, 8, 0)
    came = swap(lax.dynamic_slice_in_dim(m_d, (1 - core) * 8, 8, 0))
    w_d = jnp.stack(by_flag(core == 0, kept, came), axis=1).reshape(1280, 1024)

    d_gu, g_d, y, y_other, h2t = ffn_call(h2p, swap(h2p), dy_wide, dy_other, w_ff, w_d)
    g_d = g_d.reshape(8, 2, 80, 1024)
    kept = lax.dynamic_index_in_dim(g_d, core, 1, keepdims=False)
    came = swap(lax.dynamic_index_in_dim(g_d, 1 - core, 1, keepdims=False))
    g_d = pack_down(jnp.concatenate(by_flag(core == 0, kept, came), axis=0)).reshape(1024, 1280)
    g_ff, e_own, e_other = ffn_grad_call(h2t, d_gu, w_ff)
    g_ff = lax.dynamic_update_slice(g_ff, g_d, (0, FF))
    t_ff = lax.psum_scatter(g_ff, "shard", scatter_dimension=0, tiled=True)
    out = (mixed + y[:, :D] + swap(y_other.astype(BF)).astype(F32)[:, :D]).astype(BF)

    grad_in, qk_own, ov_own, qk_other, ov_other = kernel_call(
        backward_kernel,
        [((256, D), BF)] + [((512, QK), BF)] * 4,
        [((256, D), BF), ((256, QK), F32), ((256, QK), BF), ((256, QK), BF), ((256, QK), BF),
         ((256, D), F32)],
        16,
        8 * 10**9,
        e_own, swap(e_other), dy, mixed, h1a, h1b, att_p, qkr, values, pb, *w_qk, *w_ov,
        e_a, e_b, e_abs, cos, sin, x,
    )
    t_qk = scatter_rel(qk_own, qk_other, "z", "y")
    t_ov = scatter_rel(ov_own, ov_other, "y", "z")
    t_at = all_x(jnp.concatenate([t_qk, t_ov], axis=1))
    t_at = jnp.concatenate(by_flag(core == 0, t_at, swap(t_at)), axis=0)[:60].astype(F32)

    t_ff = sum_x(t_ff, where)
    t_ff = by_flag(core == 0, t_ff, swap(t_ff))
    columns = lambda at: jnp.concatenate(
        [t[:60, at + 512 * j : at + 512 * j + 256] for t in t_ff for j in range(5)], axis=1
    ).astype(F32)
    t_g, t_u = (columns(0), columns(256))
    t_d = jnp.concatenate([unpack_down(t[None, :, FF:])[0, :, :D] for t in t_ff], axis=0)
    t_q, t_k, t_o, t_v = (t_at[:, :D], t_at[:, D:QK], t_at[:, QK : QK + D], t_at[:, QK + D :])
    rowsum = lambda w, t: jnp.sum(w.astype(F32) * t, axis=1)
    grad_ga = rowsum(wq, t_q) + rowsum(wk, t_k) + rowsum(wv, t_v)
    grad_gf = rowsum(wg, t_g) + rowsum(wu, t_u)
    return (
        out,
        grad_in,
        t_q * ga,
        t_k * ga,
        t_v * ga,
        t_o,
        t_g * gf,
        t_u * gf,
        t_d.astype(F32),
        grad_ga,
        grad_gf,
    )


def solution(mesh):
    token = P(("rep", "shard"), None)
    row = P("shard", None)
    return jax.shard_map(
        local,
        mesh=mesh,
        in_specs=(token, P(("rep", "shard")), token) + (row,) * 7 + (P("shard"),) * 2,
        out_specs=(token, token) + (row,) * 7 + (P("shard"),) * 2,
        check_vma=False,
    )
```

```python
import jax
import jax.numpy as jnp
from jax import lax
from jax.experimental import pallas as pl
from jax.experimental.pallas import tpu as pltpu
from jax.sharding import PartitionSpec as P

H = 15
KVH = 5
HD = 64
D = 960
QK = 1280
FF = 2560
EPSILON = 1e-05
THETA = 100000.0
F32 = jnp.float32
BF = jnp.bfloat16
AX = ("rep", "shard")


def device(x, c, z, y):
    return ((x % 4) * 2 + c % 2) * 16 + (z % 4) * 4 + y % 4


def shift(value, axis, step):
    move = {"x": 0, "c": 0, "z": 0, "y": 0, axis: step}
    pairs = [
        (device(x, c, z, y), device(x + move["x"], c + move["c"], z + move["z"], y + move["y"]))
        for x in range(4)
        for c in range(2)
        for z in range(4)
        for y in range(4)
    ]
    return lax.ppermute(value, AX, pairs)


def dot(left, right):
    return jnp.dot(left, right, preferred_element_type=F32)


def dot_t(left, right):
    return lax.dot_general(left, right, (((1,), (1,)), ((), ())), preferred_element_type=F32)


def t_dot(left, right):
    return lax.dot_general(left, right, (((0,), (0,)), ((), ())), preferred_element_type=F32)


def collect(value, axis):
    return [value] + [shift(value, axis, -step) for step in (1, 2, 3)]


def spread(blocks, axis):
    got = [shift(blocks[step], axis, step) for step in (1, 2, 3)]
    total = blocks[0].astype(F32)
    for part in got:
        total = total + part.astype(F32)
    return total.astype(BF)


def place_x(blocks, where, axis):
    size = blocks[0].shape[axis]
    shape = [n * 4 if i == axis else n for i, n in enumerate(blocks[0].shape)]
    whole = jnp.zeros(shape, BF)
    for step, block in enumerate(blocks):
        start = [0] * len(shape)
        start[axis] = (where["x"] + step) % 4 * size
        whole = lax.dynamic_update_slice(whole, block, start)
    return whole


def parts_x(value, where, axis):
    size = value.shape[axis] // 4
    return [
        lax.dynamic_slice_in_dim(value, (where["x"] + step) % 4 * size, size, axis)
        for step in range(4)
    ]


def gather_rel(value, where):
    value = lax.dynamic_slice_in_dim(value, where["x"] * 640, 640, 1)
    value = jnp.concatenate(collect(value, "y"), axis=0)
    value = jnp.concatenate(collect(value, "z"), axis=0)
    mine = place_x(collect(value, "x"), where, 1)
    return [mine, swap(mine)]


def scatter_rel(own, other, where):
    total = (own.astype(F32) + swap(other).astype(F32)).astype(BF)
    total = spread(parts_x(total, where, 1), "x")
    for axis in ("z", "y"):
        rows = total.shape[0] // 4
        total = spread([total[i * rows : (i + 1) * rows] for i in range(4)], axis)
    return place_x(collect(total, "x"), where, 1)


def swap(value):
    return shift(value, "c", 1)


def sum_x(part, where):
    return place_x(collect(spread(parts_x(part, where, 0), "x"), "x"), where, 0)


def by_flag(low, mine, other):
    return (jnp.where(low, mine, other), jnp.where(low, other, mine))


def pack_down(value):
    last = value[:, 64:]
    tail = jnp.concatenate([last[:, :, i * 256 : (i + 1) * 256] for i in range(4)], axis=1)
    return jnp.concatenate([value[:, :64], tail], axis=2)


def unpack_down(value):
    tail = value[:, :, 1024:]
    last = jnp.concatenate([tail[:, i * 16 : (i + 1) * 16] for i in range(4)], axis=2)
    return jnp.concatenate([value[:, :, :1024], last], axis=1)


def order_rel(where):
    place = lax.broadcasted_iota(jnp.int32, (D, 1024), 1)
    natural = lax.broadcasted_iota(jnp.int32, (D, 1024), 0)
    core = (where["c"] + place // 512) % 2
    z = (where["z"] + (place // 128) % 4) % 4
    y = (where["y"] + (place // 32) % 4) % 4
    inner = core * 32 + place % 32
    return (((z * 4 + y) * 60 + inner == natural) & (inner < 60)).astype(BF)


def order_abs():
    place = lax.broadcasted_iota(jnp.int32, (D, 1024), 1)
    natural = lax.broadcasted_iota(jnp.int32, (D, 1024), 0)
    inner = place % 64
    return (((place // 64) * 60 + inner == natural) & (inner < 60)).astype(BF)


def rotary_tables(segments):
    count = segments.shape[0]
    index = jnp.arange(count, dtype=jnp.int32)
    same = segments[:, None] == segments[None, :]
    first = jnp.min(jnp.where(same, index[None, :], count), axis=-1)
    position = (index - first).astype(F32)
    half = HD // 2
    freq = THETA ** (-jnp.arange(half, dtype=F32) / half)
    angle = position[:, None] * freq
    cos, sin = (jnp.cos(angle), jnp.sin(angle))
    return (
        jnp.concatenate([cos] * 4, axis=1),
        jnp.concatenate([-sin, sin, -sin, sin], axis=1),
    )


def norm(values):
    scale = lax.rsqrt(jnp.mean(values * values, axis=-1, keepdims=True) + EPSILON)
    return (values * scale, scale)


def norm_back(e, normed, scale):
    return scale * (e - normed * jnp.mean(e * normed, axis=-1, keepdims=True))


def swap_halves(block):
    lane = lax.broadcasted_iota(jnp.int32, block.shape, 1)
    return jnp.where(lane % 64 < 32, pltpu.roll(block, 96, 1), pltpu.roll(block, 32, 1))


def forward_kernel(
    x_ref, h1_ref, w_ref, w2_ref, erel_ref, eabs_ref, cos_ref, sin_ref, segc_ref,
    segr_ref,
    qkr_ref, v_ref, pb_ref, attp_ref, mixed_ref, h2p_ref, att_ref,
):
    cos, sin = (cos_ref[...], sin_ref[...])
    for i in range(10):
        lanes = slice(128 * i, 128 * i + 128)
        part = dot(h1_ref[:, :512], w_ref[:, lanes]) + dot(h1_ref[:, 512:], w2_ref[:, lanes])
        qkr_ref[:, lanes] = (part * cos + swap_halves(part) * sin).astype(BF)
    v_ref[...] = (
        dot(h1_ref[:, :512], w_ref[:, 2176:]) + dot(h1_ref[:, 512:], w2_ref[:, 2176:])
    ).astype(BF)
    row = lax.broadcasted_iota(jnp.int32, (256, 256), 0)
    col = lax.broadcasted_iota(jnp.int32, (256, 256), 1)
    allowed = (segc_ref[...] == segr_ref[...]) & (row >= col)
    for h in range(H):
        g = h // 3
        q = qkr_ref[:, 64 * h : 64 * h + 64]
        k = qkr_ref[:, D + 64 * g : D + 64 * g + 64]
        scores = jnp.where(allowed, dot_t(q, k) * 0.125, -1e30)
        weight = jnp.exp(scores - jnp.max(scores, axis=-1, keepdims=True))
        pb = (weight / jnp.sum(weight, axis=-1, keepdims=True)).astype(BF)
        pb_ref[h] = pb
        att_ref[:, 64 * h : 64 * h + 64] = dot(pb, v_ref[:, 64 + 64 * g : 128 + 64 * g]).astype(BF)
    att_p = dot(att_ref[...], erel_ref[...]).astype(BF)
    attp_ref[...] = att_p
    mixed = (
        x_ref[...].astype(F32)
        + dot(att_p[:, :512], w_ref[:, QK : QK + D])
        + dot(att_p[:, 512:], w2_ref[:, QK : QK + D])
    )
    mixed_ref[...] = mixed
    h2p_ref[...] = dot(norm(mixed)[0].astype(BF), eabs_ref[...]).astype(BF)


def ffn_kernel(
    h2a_ref, h2b_ref, dya_ref, dyb_ref, wg_ref, wu_ref, wd_ref,
    dgu_ref, gd_ref, ya_ref, yb_ref, h2t_ref, h2_ref, dy_ref,
):
    @pl.when(pl.program_id(0) == 0)
    def _():
        h2_ref[:256] = h2a_ref[...]
        h2_ref[256:] = h2b_ref[...]
        dy_ref[:256] = dya_ref[...]
        dy_ref[256:] = dyb_ref[...]
        h2t_ref[...] = h2_ref[...].T
        ya_ref[...] = jnp.zeros_like(ya_ref)
        yb_ref[...] = jnp.zeros_like(yb_ref)

    h2, dy, wd = (h2_ref[...], dy_ref[...], wd_ref[...])
    gate, up, d_act = (dot(h2, wg_ref[...]), dot(h2, wu_ref[...]), dot_t(dy, wd))
    sig = jax.nn.sigmoid(gate)
    silu = gate * sig
    act = (silu * up).astype(BF)
    dgu_ref[:, :256] = (d_act * up * sig * (1.0 + gate * (1.0 - sig))).astype(BF)
    dgu_ref[:, 256:] = (d_act * silu).astype(BF)
    gd_ref[...] = dot(act.T, dy).astype(BF)
    ya_ref[...] += dot(act[:256], wd)
    yb_ref[...] += dot(act[256:], wd)


def ffn_grad_kernel(h2t_ref, dgu_ref, wg_ref, wu_ref, gg_ref, ea_ref, eb_ref, total_ref):
    j = pl.program_id(0)

    @pl.when(j == 0)
    def _():
        total_ref[...] = jnp.zeros_like(total_ref)

    dgu = dgu_ref[...]
    gg_ref[...] = dot(h2t_ref[...], dgu).astype(BF)
    total_ref[...] += dot_t(dgu[:, :256], wg_ref[...]) + dot_t(dgu[:, 256:], wu_ref[...])

    @pl.when(j == 4)
    def _():
        ea_ref[...] = total_ref[:256]
        eb_ref[...] = total_ref[256:].astype(BF)


def backward_kernel(
    ef_ref, came_ref, dy_ref, mixed_ref, h1_ref, attp_ref, qkr_ref, v_ref, pb_ref,
    w_ref, w2_ref, erel_ref, eabs_ref, cos_ref, sin_ref, x_ref,
    gin_ref, own_ref, other_ref,
    dob_ref, raw_ref, da_ref, dqk_ref, dv_ref, dmixed_ref,
):
    e = dot_t((ef_ref[...] + came_ref[...].astype(F32)).astype(BF), eabs_ref[...])
    n2, r2 = norm(mixed_ref[...])
    d_mixed = dy_ref[...].astype(F32) + norm_back(e, n2, r2)
    dmixed_ref[...] = d_mixed
    d_attn = d_mixed.astype(BF)
    da_ref[:, :D] = d_attn
    da_ref[:, D:] = jnp.zeros((256, 320), BF)
    dob_ref[...] = (
        dot_t(dot_t(d_attn, w_ref[:, QK : QK + D]).astype(BF), erel_ref[:, :512])
        + dot_t(dot_t(d_attn, w2_ref[:, QK : QK + D]).astype(BF), erel_ref[:, 512:])
    ).astype(BF)
    dv_ref[:, :D] = jnp.zeros((256, D), BF)
    for g in range(KVH):
        k = qkr_ref[:, D + 64 * g : D + 64 * g + 64]
        v = v_ref[:, 64 + 64 * g : 128 + 64 * g]
        d_v = jnp.zeros((256, HD), F32)
        d_k = jnp.zeros((256, HD), F32)
        for h in range(3 * g, 3 * g + 3):
            pb = pb_ref[h]
            d_ob = dob_ref[:, 64 * h : 64 * h + 64]
            d_p = dot_t(d_ob, v)
            probs = pb.astype(F32)
            row_dot = jnp.sum(probs * d_p, axis=-1, keepdims=True)
            d_s = (probs * (d_p - row_dot) * 0.125).astype(BF)
            raw_ref[:, 64 * h : 64 * h + 64] = dot(d_s, k)
            d_v += t_dot(pb, d_ob)
            d_k += t_dot(d_s, qkr_ref[:, 64 * h : 64 * h + 64])
        raw_ref[:, D + 64 * g : D + 64 * g + 64] = d_k
        dv_ref[:, D + 64 * g : D + 64 * g + 64] = d_v.astype(BF)
    cos, sin = (cos_ref[...], sin_ref[...])
    for i in range(10):
        lanes = slice(128 * i, 128 * i + 128)
        part = raw_ref[:, lanes]
        dqk_ref[:, lanes] = (part * cos - swap_halves(part) * sin).astype(BF)
    for ref, rows in ((other_ref, slice(512, 1024)), (own_ref, slice(0, 512))):
        h1t = h1_ref[:, rows].T
        ref[:, :QK] = dot(h1t, dqk_ref[...]).astype(BF)
        ref[:, QK:] = (dot(attp_ref[:, rows].T, da_ref[...]) + dot(h1t, dv_ref[...])).astype(BF)
    e = 0.0
    for ref, rows in ((w_ref, slice(0, 512)), (w2_ref, slice(512, 1024))):
        part = dot_t(dqk_ref[...], ref[:, :QK]) + dot_t(dv_ref[:, 896:], ref[:, 2176:])
        e = e + dot_t(part.astype(BF), erel_ref[:, rows])
    n1, r1 = norm(x_ref[...].astype(F32))
    gin_ref[...] = (dmixed_ref[...] + norm_back(e, n1, r1)).astype(BF)


def kernel_call(kernel, outs, scratch, mib, flops, *args):
    whole = pl.BlockSpec(memory_space=pltpu.VMEM)
    shapes = [jax.ShapeDtypeStruct(*out) for out in outs]
    size = sum(s.size * s.dtype.itemsize for s in list(args) + shapes)
    return pl.pallas_call(
        kernel,
        out_shape=shapes,
        in_specs=[whole] * len(args),
        out_specs=[whole] * len(outs),
        scratch_shapes=[pltpu.VMEM(*s) for s in scratch],
        compiler_params=pltpu.CompilerParams(vmem_limit_bytes=mib * 2**20),
        cost_estimate=pl.CostEstimate(flops=flops, bytes_accessed=size, transcendentals=0),
    )(*args)


def in_hbm(value):
    return pltpu.with_memory_space_constraint(value, pltpu.HBM)


def ffn_call(h2a, h2b, dya, dyb, w_ff, w_d):
    fixed = lambda j: (0, 0)
    token = pl.BlockSpec((256, 1024), fixed)
    return pl.pallas_call(
        ffn_kernel,
        grid=(5,),
        out_shape=[
            pltpu.HBM((512, 2560), BF),
            jax.ShapeDtypeStruct((1280, 1024), BF),
            pltpu.HBM((256, 1024), F32),
            pltpu.HBM((256, 1024), F32),
            pltpu.HBM((1024, 512), BF),
        ],
        in_specs=[token] * 4
        + [
            pl.BlockSpec((1024, 256), lambda j: (0, j)),
            pl.BlockSpec((1024, 256), lambda j: (0, 5 + j)),
            pl.BlockSpec((256, 1024), lambda j: (j, 0)),
        ],
        out_specs=[
            pl.BlockSpec((512, 512), lambda j: (0, j)),
            pl.BlockSpec((256, 1024), lambda j: (j, 0)),
            token,
            token,
            pl.BlockSpec((1024, 512), fixed),
        ],
        scratch_shapes=[pltpu.VMEM((512, 1024), BF), pltpu.VMEM((512, 1024), BF)],
        compiler_params=pltpu.CompilerParams(vmem_limit_bytes=22 * 2**20),
        cost_estimate=pl.CostEstimate(
            flops=7 * 10**9, bytes_accessed=20 * 10**6, transcendentals=512 * 1280
        ),
    )(in_hbm(h2a), in_hbm(h2b), in_hbm(dya), in_hbm(dyb), in_hbm(w_ff), in_hbm(w_ff), w_d)


def ffn_grad_call(h2t, dgu, w_ff):
    fixed = lambda j: (0, 0)
    token = pl.BlockSpec((256, 1024), fixed)
    return pl.pallas_call(
        ffn_grad_kernel,
        grid=(5,),
        out_shape=[
            pltpu.HBM((1024, 3840), BF),
            pltpu.HBM((256, 1024), F32),
            pltpu.HBM((256, 1024), BF),
        ],
        in_specs=[
            pl.BlockSpec((1024, 512), fixed),
            pl.BlockSpec((512, 512), lambda j: (0, j)),
            pl.BlockSpec((1024, 256), lambda j: (0, j)),
            pl.BlockSpec((1024, 256), lambda j: (0, 5 + j)),
        ],
        out_specs=[pl.BlockSpec((1024, 512), lambda j: (0, j)), token, token],
        scratch_shapes=[pltpu.VMEM((512, 1024), F32)],
        compiler_params=pltpu.CompilerParams(vmem_limit_bytes=18 * 2**20),
        cost_estimate=pl.CostEstimate(
            flops=6 * 10**9, bytes_accessed=16 * 10**6, transcendentals=0
        ),
    )(in_hbm(h2t), in_hbm(dgu), in_hbm(w_ff), in_hbm(w_ff))


def local(x, seg, dy, wq, wk, wv, wo, wg, wu, wd, gain_a, gain_f):
    rep = lax.axis_index("rep")
    shard = lax.axis_index("shard")
    where = {"x": rep // 2, "c": rep % 2, "z": shard // 4, "y": shard % 4}
    core = where["c"]
    ga = gain_a[:, None]
    gf = gain_f[:, None]
    scaled = lambda w, g: (w.astype(F32) * g).astype(BF)
    tall = lambda w: jnp.pad(w, ((0, 4), (0, 0)))
    s_at = tall(jnp.concatenate([scaled(wq, ga), scaled(wk, ga), wo, scaled(wv, ga)], axis=1))
    w_at = gather_rel(lax.dynamic_slice_in_dim(s_at, core * 32, 32, 0), where)
    half = lambda w: lax.dynamic_slice_in_dim(w, core * 1280, 1280, 1)
    s_d = jnp.pad(lax.dynamic_slice_in_dim(wd, core * 80, 80, 0), ((0, 0), (0, 64)))
    s_ff = jnp.concatenate(
        [tall(scaled(half(wg), gf)), tall(scaled(half(wu), gf)), pack_down(s_d[None])[0]], axis=1
    )
    w_ff = lax.all_gather(s_ff, "shard", axis=0, tiled=True)
    e_rel = order_rel(where)
    e_abs = order_abs()
    dy_wide = jnp.pad(dy, ((0, 0), (0, 64)))
    dy_other = swap(dy_wide)

    n1 = norm(x.astype(F32))[0]
    h1 = dot(n1.astype(BF), e_rel).astype(BF)
    cos, sin = rotary_tables(seg)
    qkr, values, pb, att_p, mixed, h2p = kernel_call(
        forward_kernel,
        [((256, QK), BF), ((256, 384), BF), ((H, 256, 256), BF), ((256, 1024), BF),
         ((256, D), F32), ((256, 1024), BF)],
        [((256, D), BF)],
        12,
        4 * 10**9,
        x, h1, *w_at, e_rel, e_abs, cos, sin, seg[:, None], seg[None, :],
    )

    w_ff, h2p = lax.optimization_barrier((w_ff, h2p))
    m_d = unpack_down(w_ff[:, FF:].reshape(16, 64, 1280))
    kept = lax.dynamic_slice_in_dim(m_d, core * 8, 8, 0)
    came = swap(lax.dynamic_slice_in_dim(m_d, (1 - core) * 8, 8, 0))
    w_d = jnp.stack(by_flag(core == 0, kept, came), axis=1).reshape(1280, 1024)

    d_gu, g_d, y, y_other, h2t = ffn_call(h2p, swap(h2p), dy_wide, dy_other, w_ff, w_d)
    g_d = g_d.reshape(8, 2, 80, 1024)
    kept = lax.dynamic_index_in_dim(g_d, core, 1, keepdims=False)
    came = swap(lax.dynamic_index_in_dim(g_d, 1 - core, 1, keepdims=False))
    g_d = pack_down(jnp.concatenate(by_flag(core == 0, kept, came), axis=0)).reshape(1024, 1280)
    g_ff, e_own, e_other = ffn_grad_call(h2t, d_gu, w_ff)
    g_ff = lax.dynamic_update_slice(g_ff, g_d, (0, FF))
    t_ff = lax.psum_scatter(g_ff, "shard", scatter_dimension=0, tiled=True)
    out = (mixed + y[:, :D] + swap(y_other.astype(BF)).astype(F32)[:, :D]).astype(BF)

    grad_in, g_own, g_other = kernel_call(
        backward_kernel,
        [((256, D), BF), ((512, 2 * QK), BF), ((512, 2 * QK), BF)],
        [((256, D), BF), ((256, QK), F32), ((256, QK), BF), ((256, QK), BF), ((256, QK), BF),
         ((256, D), F32)],
        16,
        8 * 10**9,
        e_own, swap(e_other), dy, mixed, h1, att_p, qkr, values, pb, *w_at,
        e_rel, e_abs, cos, sin, x,
    )
    t_at = scatter_rel(g_own, g_other, where)
    t_at = jnp.concatenate(by_flag(core == 0, t_at, swap(t_at)), axis=0)[:60].astype(F32)

    t_ff = sum_x(t_ff, where)
    t_ff = by_flag(core == 0, t_ff, swap(t_ff))
    columns = lambda at: jnp.concatenate(
        [t[:60, at + 512 * j : at + 512 * j + 256] for t in t_ff for j in range(5)], axis=1
    ).astype(F32)
    t_g, t_u = (columns(0), columns(256))
    t_d = jnp.concatenate([unpack_down(t[None, :, FF:])[0, :, :D] for t in t_ff], axis=0)
    t_q, t_k, t_o, t_v = (t_at[:, :D], t_at[:, D:QK], t_at[:, QK : QK + D], t_at[:, QK + D :])
    rowsum = lambda w, t: jnp.sum(w.astype(F32) * t, axis=1)
    grad_ga = rowsum(wq, t_q) + rowsum(wk, t_k) + rowsum(wv, t_v)
    grad_gf = rowsum(wg, t_g) + rowsum(wu, t_u)
    return (
        out,
        grad_in,
        t_q * ga,
        t_k * ga,
        t_v * ga,
        t_o,
        t_g * gf,
        t_u * gf,
        t_d.astype(F32),
        grad_ga,
        grad_gf,
    )


def solution(mesh):
    token = P(("rep", "shard"), None)
    row = P("shard", None)
    return jax.shard_map(
        local,
        mesh=mesh,
        in_specs=(token, P(("rep", "shard")), token) + (row,) * 7 + (P("shard"),) * 2,
        out_specs=(token, token) + (row,) * 7 + (P("shard"),) * 2,
        check_vma=False,
    )
```

```python
import jax
import jax.numpy as jnp
from jax import lax
from jax.experimental import pallas as pl
from jax.experimental.pallas import tpu as pltpu
from jax.sharding import PartitionSpec as P

H = 15
KVH = 5
HD = 64
D = 960
QK = 1280
FF = 2560
EPSILON = 1e-05
THETA = 100000.0
F32 = jnp.float32
BF = jnp.bfloat16
AX = ("rep", "shard")


def device(x, c, z, y):
    return ((x % 4) * 2 + c % 2) * 16 + (z % 4) * 4 + y % 4


def shift(value, axis, step):
    move = {"x": 0, "c": 0, "z": 0, "y": 0, axis: step}
    pairs = [
        (device(x, c, z, y), device(x + move["x"], c + move["c"], z + move["z"], y + move["y"]))
        for x in range(4)
        for c in range(2)
        for z in range(4)
        for y in range(4)
    ]
    return lax.ppermute(value, AX, pairs)


def dot(left, right):
    return jnp.dot(left, right, preferred_element_type=F32)


def dot_t(left, right):
    return lax.dot_general(left, right, (((1,), (1,)), ((), ())), preferred_element_type=F32)


def t_dot(left, right):
    return lax.dot_general(left, right, (((0,), (0,)), ((), ())), preferred_element_type=F32)


def collect(value, axis):
    return [value] + [shift(value, axis, -step) for step in (1, 2, 3)]


def spread(blocks, axis):
    got = [shift(blocks[step], axis, step) for step in (1, 2, 3)]
    total = blocks[0].astype(F32)
    for part in got:
        total = total + part.astype(F32)
    return total.astype(BF)


def place_x(blocks, where, axis):
    size = blocks[0].shape[axis]
    shape = [n * 4 if i == axis else n for i, n in enumerate(blocks[0].shape)]
    whole = jnp.zeros(shape, BF)
    for step, block in enumerate(blocks):
        start = [0] * len(shape)
        start[axis] = (where["x"] + step) % 4 * size
        whole = lax.dynamic_update_slice(whole, block, start)
    return whole


def parts_x(value, where, axis):
    size = value.shape[axis] // 4
    return [
        lax.dynamic_slice_in_dim(value, (where["x"] + step) % 4 * size, size, axis)
        for step in range(4)
    ]


def gather_rel(value, where):
    value = lax.dynamic_slice_in_dim(value, where["x"] * 640, 640, 1)
    value = jnp.concatenate(collect(value, "y"), axis=0)
    value = jnp.concatenate(collect(value, "z"), axis=0)
    mine = place_x(collect(value, "x"), where, 1)
    return [mine, swap(mine)]


def scatter_rel(own, other, where):
    total = (own.astype(F32) + swap(other).astype(F32)).astype(BF)
    total = spread(parts_x(total, where, 1), "x")
    for axis in ("z", "y"):
        rows = total.shape[0] // 4
        total = spread([total[i * rows : (i + 1) * rows] for i in range(4)], axis)
    return place_x(collect(total, "x"), where, 1)


def swap(value):
    return shift(value, "c", 1)


def sum_x(part, where):
    return place_x(collect(spread(parts_x(part, where, 0), "x"), "x"), where, 0)


def by_flag(low, mine, other):
    return (jnp.where(low, mine, other), jnp.where(low, other, mine))


def pack_down(value):
    last = value[:, 64:]
    tail = jnp.concatenate([last[:, :, i * 256 : (i + 1) * 256] for i in range(4)], axis=1)
    return jnp.concatenate([value[:, :64], tail], axis=2)


def unpack_down(value):
    tail = value[:, :, 1024:]
    last = jnp.concatenate([tail[:, i * 16 : (i + 1) * 16] for i in range(4)], axis=2)
    return jnp.concatenate([value[:, :, :1024], last], axis=1)


def order_rel(where):
    place = lax.broadcasted_iota(jnp.int32, (D, 1024), 1)
    natural = lax.broadcasted_iota(jnp.int32, (D, 1024), 0)
    core = (where["c"] + place // 512) % 2
    z = (where["z"] + (place // 128) % 4) % 4
    y = (where["y"] + (place // 32) % 4) % 4
    inner = core * 32 + place % 32
    return (((z * 4 + y) * 60 + inner == natural) & (inner < 60)).astype(BF)


def order_abs():
    place = lax.broadcasted_iota(jnp.int32, (D, 1024), 1)
    natural = lax.broadcasted_iota(jnp.int32, (D, 1024), 0)
    inner = place % 64
    return (((place // 64) * 60 + inner == natural) & (inner < 60)).astype(BF)


def rotary_tables(segments):
    count = segments.shape[0]
    index = jnp.arange(count, dtype=jnp.int32)
    same = segments[:, None] == segments[None, :]
    first = jnp.min(jnp.where(same, index[None, :], count), axis=-1)
    position = (index - first).astype(F32)
    half = HD // 2
    freq = THETA ** (-jnp.arange(half, dtype=F32) / half)
    angle = position[:, None] * freq
    cos, sin = (jnp.cos(angle), jnp.sin(angle))
    return (
        jnp.concatenate([cos] * 4, axis=1),
        jnp.concatenate([-sin, sin, -sin, sin], axis=1),
    )


def norm(values):
    scale = lax.rsqrt(jnp.mean(values * values, axis=-1, keepdims=True) + EPSILON)
    return (values * scale, scale)


def norm_back(e, normed, scale):
    return scale * (e - normed * jnp.mean(e * normed, axis=-1, keepdims=True))


def swap_halves(block):
    lane = lax.broadcasted_iota(jnp.int32, block.shape, 1)
    return jnp.where(lane % 64 < 32, pltpu.roll(block, 96, 1), pltpu.roll(block, 32, 1))


def forward_kernel(
    x_ref, h1_ref, w_ref, w2_ref, erel_ref, eabs_ref, cos_ref, sin_ref, segc_ref,
    segr_ref,
    qkr_ref, v_ref, pb_ref, attp_ref, mixed_ref, h2p_ref, att_ref,
):
    cos, sin = (cos_ref[...], sin_ref[...])
    for i in range(10):
        lanes = slice(128 * i, 128 * i + 128)
        part = dot(h1_ref[:, :512], w_ref[:, lanes]) + dot(h1_ref[:, 512:], w2_ref[:, lanes])
        qkr_ref[:, lanes] = (part * cos + swap_halves(part) * sin).astype(BF)
    v_ref[...] = (
        dot(h1_ref[:, :512], w_ref[:, 2176:]) + dot(h1_ref[:, 512:], w2_ref[:, 2176:])
    ).astype(BF)
    row = lax.broadcasted_iota(jnp.int32, (256, 256), 0)
    col = lax.broadcasted_iota(jnp.int32, (256, 256), 1)
    allowed = (segc_ref[...] == segr_ref[...]) & (row >= col)
    for h in range(H):
        g = h // 3
        q = qkr_ref[:, 64 * h : 64 * h + 64]
        k = qkr_ref[:, D + 64 * g : D + 64 * g + 64]
        scores = jnp.where(allowed, dot_t(q, k) * 0.125, -1e30)
        weight = jnp.exp(scores - jnp.max(scores, axis=-1, keepdims=True))
        pb = (weight / jnp.sum(weight, axis=-1, keepdims=True)).astype(BF)
        pb_ref[h] = pb
        att_ref[:, 64 * h : 64 * h + 64] = dot(pb, v_ref[:, 64 + 64 * g : 128 + 64 * g]).astype(BF)
    att_p = dot(att_ref[...], erel_ref[...]).astype(BF)
    attp_ref[...] = att_p
    mixed = (
        x_ref[...].astype(F32)
        + dot(att_p[:, :512], w_ref[:, QK : QK + D])
        + dot(att_p[:, 512:], w2_ref[:, QK : QK + D])
    )
    mixed_ref[...] = mixed
    h2p_ref[...] = dot(norm(mixed)[0].astype(BF), eabs_ref[...]).astype(BF)


def ffn_kernel(
    h2a_ref, h2b_ref, dya_ref, dyb_ref, wg_ref, wu_ref, wd_ref,
    dgu_ref, gd_ref, ya_ref, yb_ref, h2t_ref, h2_ref, dy_ref,
):
    @pl.when(pl.program_id(0) == 0)
    def _():
        h2_ref[:256] = h2a_ref[...]
        h2_ref[256:] = h2b_ref[...]
        dy_ref[:256] = dya_ref[...]
        dy_ref[256:] = dyb_ref[...]
        h2t_ref[...] = h2_ref[...].T
        ya_ref[...] = jnp.zeros_like(ya_ref)
        yb_ref[...] = jnp.zeros_like(yb_ref)

    h2, dy, wd = (h2_ref[...], dy_ref[...], wd_ref[...])
    gate, up, d_act = (dot(h2, wg_ref[...]), dot(h2, wu_ref[...]), dot_t(dy, wd))
    sig = jax.nn.sigmoid(gate)
    silu = gate * sig
    act = (silu * up).astype(BF)
    dgu_ref[:, :256] = (d_act * up * sig * (1.0 + gate * (1.0 - sig))).astype(BF)
    dgu_ref[:, 256:] = (d_act * silu).astype(BF)
    gd_ref[...] = dot(act.T, dy).astype(BF)
    ya_ref[...] += dot(act[:256], wd)
    yb_ref[...] += dot(act[256:], wd)


def ffn_grad_kernel(h2t_ref, dgu_ref, wg_ref, wu_ref, gg_ref, ea_ref, eb_ref, total_ref):
    j = pl.program_id(0)

    @pl.when(j == 0)
    def _():
        total_ref[...] = jnp.zeros_like(total_ref)

    dgu = dgu_ref[...]
    gg_ref[...] = dot(h2t_ref[...], dgu).astype(BF)
    total_ref[...] += dot_t(dgu[:, :256], wg_ref[...]) + dot_t(dgu[:, 256:], wu_ref[...])

    @pl.when(j == 4)
    def _():
        ea_ref[...] = total_ref[:256]
        eb_ref[...] = total_ref[256:].astype(BF)


def backward_kernel(
    ef_ref, came_ref, dy_ref, mixed_ref, h1_ref, attp_ref, qkr_ref, v_ref, pb_ref,
    w_ref, w2_ref, erel_ref, eabs_ref, cos_ref, sin_ref, x_ref,
    gin_ref, own_ref, other_ref,
    dob_ref, raw_ref, da_ref, dqk_ref, dv_ref, dmixed_ref,
):
    e = dot_t((ef_ref[...] + came_ref[...].astype(F32)).astype(BF), eabs_ref[...])
    n2, r2 = norm(mixed_ref[...])
    d_mixed = dy_ref[...].astype(F32) + norm_back(e, n2, r2)
    dmixed_ref[...] = d_mixed
    d_attn = d_mixed.astype(BF)
    da_ref[:, :D] = d_attn
    da_ref[:, D:] = jnp.zeros((256, 320), BF)
    dob_ref[...] = (
        dot_t(dot_t(d_attn, w_ref[:, QK : QK + D]).astype(BF), erel_ref[:, :512])
        + dot_t(dot_t(d_attn, w2_ref[:, QK : QK + D]).astype(BF), erel_ref[:, 512:])
    ).astype(BF)
    dv_ref[:, :D] = jnp.zeros((256, D), BF)
    for g in range(KVH):
        k = qkr_ref[:, D + 64 * g : D + 64 * g + 64]
        v = v_ref[:, 64 + 64 * g : 128 + 64 * g]
        d_v = jnp.zeros((256, HD), F32)
        d_k = jnp.zeros((256, HD), F32)
        for h in range(3 * g, 3 * g + 3):
            pb = pb_ref[h]
            d_ob = dob_ref[:, 64 * h : 64 * h + 64]
            d_p = dot_t(d_ob, v)
            probs = pb.astype(F32)
            row_dot = jnp.sum(probs * d_p, axis=-1, keepdims=True)
            d_s = (probs * (d_p - row_dot) * 0.125).astype(BF)
            raw_ref[:, 64 * h : 64 * h + 64] = dot(d_s, k)
            d_v += t_dot(pb, d_ob)
            d_k += t_dot(d_s, qkr_ref[:, 64 * h : 64 * h + 64])
        raw_ref[:, D + 64 * g : D + 64 * g + 64] = d_k
        dv_ref[:, D + 64 * g : D + 64 * g + 64] = d_v.astype(BF)
    cos, sin = (cos_ref[...], sin_ref[...])
    for i in range(10):
        lanes = slice(128 * i, 128 * i + 128)
        part = raw_ref[:, lanes]
        dqk_ref[:, lanes] = (part * cos - swap_halves(part) * sin).astype(BF)
    for ref, rows in ((other_ref, slice(512, 1024)), (own_ref, slice(0, 512))):
        h1t = h1_ref[:, rows].T
        ref[:, :QK] = dot(h1t, dqk_ref[...]).astype(BF)
        ref[:, QK:] = (dot(attp_ref[:, rows].T, da_ref[...]) + dot(h1t, dv_ref[...])).astype(BF)
    e = 0.0
    for ref, rows in ((w_ref, slice(0, 512)), (w2_ref, slice(512, 1024))):
        part = dot_t(dqk_ref[...], ref[:, :QK]) + dot_t(dv_ref[:, 896:], ref[:, 2176:])
        e = e + dot_t(part.astype(BF), erel_ref[:, rows])
    n1, r1 = norm(x_ref[...].astype(F32))
    gin_ref[...] = (dmixed_ref[...] + norm_back(e, n1, r1)).astype(BF)


def in_hbm(value):
    return pltpu.with_memory_space_constraint(value, pltpu.HBM)


def kernel_call(kernel, outs, scratch, mib, flops, *args):
    spec = lambda a: pl.BlockSpec(
        a.shape, lambda i: (0,) * len(a.shape), pipeline_mode=pl.Buffered(1)
    )
    shapes = [jax.ShapeDtypeStruct(*out) for out in outs]
    size = sum(s.size * s.dtype.itemsize for s in list(args) + shapes)
    return pl.pallas_call(
        kernel,
        grid=(1,),
        out_shape=[pltpu.HBM(*out) for out in outs],
        in_specs=[spec(a) for a in args],
        out_specs=[spec(a) for a in shapes],
        scratch_shapes=[pltpu.VMEM(*s) for s in scratch],
        compiler_params=pltpu.CompilerParams(vmem_limit_bytes=mib * 2**20),
        cost_estimate=pl.CostEstimate(flops=flops, bytes_accessed=size, transcendentals=0),
    )(*[in_hbm(a) for a in args])


def ffn_call(h2a, h2b, dya, dyb, w_ff, w_d):
    fixed = lambda j: (0, 0)
    token = pl.BlockSpec((256, 1024), fixed)
    return pl.pallas_call(
        ffn_kernel,
        grid=(5,),
        out_shape=[
            pltpu.HBM((512, 2560), BF),
            jax.ShapeDtypeStruct((1280, 1024), BF),
            pltpu.HBM((256, 1024), F32),
            pltpu.HBM((256, 1024), F32),
            pltpu.HBM((1024, 512), BF),
        ],
        in_specs=[token] * 4
        + [
            pl.BlockSpec((1024, 256), lambda j: (0, j)),
            pl.BlockSpec((1024, 256), lambda j: (0, 5 + j)),
            pl.BlockSpec((256, 1024), lambda j: (j, 0)),
        ],
        out_specs=[
            pl.BlockSpec((512, 512), lambda j: (0, j)),
            pl.BlockSpec((256, 1024), lambda j: (j, 0)),
            token,
            token,
            pl.BlockSpec((1024, 512), fixed),
        ],
        scratch_shapes=[pltpu.VMEM((512, 1024), BF), pltpu.VMEM((512, 1024), BF)],
        compiler_params=pltpu.CompilerParams(vmem_limit_bytes=22 * 2**20),
        cost_estimate=pl.CostEstimate(
            flops=7 * 10**9, bytes_accessed=20 * 10**6, transcendentals=512 * 1280
        ),
    )(in_hbm(h2a), in_hbm(h2b), in_hbm(dya), in_hbm(dyb), in_hbm(w_ff), in_hbm(w_ff), w_d)


def ffn_grad_call(h2t, dgu, w_ff):
    fixed = lambda j: (0, 0)
    token = pl.BlockSpec((256, 1024), fixed)
    return pl.pallas_call(
        ffn_grad_kernel,
        grid=(5,),
        out_shape=[
            pltpu.HBM((1024, 3840), BF),
            pltpu.HBM((256, 1024), F32),
            pltpu.HBM((256, 1024), BF),
        ],
        in_specs=[
            pl.BlockSpec((1024, 512), fixed),
            pl.BlockSpec((512, 512), lambda j: (0, j)),
            pl.BlockSpec((1024, 256), lambda j: (0, j)),
            pl.BlockSpec((1024, 256), lambda j: (0, 5 + j)),
        ],
        out_specs=[pl.BlockSpec((1024, 512), lambda j: (0, j)), token, token],
        scratch_shapes=[pltpu.VMEM((512, 1024), F32)],
        compiler_params=pltpu.CompilerParams(vmem_limit_bytes=18 * 2**20),
        cost_estimate=pl.CostEstimate(
            flops=6 * 10**9, bytes_accessed=16 * 10**6, transcendentals=0
        ),
    )(in_hbm(h2t), in_hbm(dgu), in_hbm(w_ff), in_hbm(w_ff))


def local(x, seg, dy, wq, wk, wv, wo, wg, wu, wd, gain_a, gain_f):
    rep = lax.axis_index("rep")
    shard = lax.axis_index("shard")
    where = {"x": rep // 2, "c": rep % 2, "z": shard // 4, "y": shard % 4}
    core = where["c"]
    ga = gain_a[:, None]
    gf = gain_f[:, None]
    scaled = lambda w, g: (w.astype(F32) * g).astype(BF)
    tall = lambda w: jnp.pad(w, ((0, 4), (0, 0)))
    s_at = tall(jnp.concatenate([scaled(wq, ga), scaled(wk, ga), wo, scaled(wv, ga)], axis=1))
    w_at = gather_rel(lax.dynamic_slice_in_dim(s_at, core * 32, 32, 0), where)
    half = lambda w: lax.dynamic_slice_in_dim(w, core * 1280, 1280, 1)
    s_d = jnp.pad(lax.dynamic_slice_in_dim(wd, core * 80, 80, 0), ((0, 0), (0, 64)))
    s_ff = jnp.concatenate(
        [tall(scaled(half(wg), gf)), tall(scaled(half(wu), gf)), pack_down(s_d[None])[0]], axis=1
    )
    w_ff = lax.all_gather(s_ff, "shard", axis=0, tiled=True)
    e_rel = order_rel(where)
    e_abs = order_abs()
    dy_wide = jnp.pad(dy, ((0, 0), (0, 64)))
    dy_other = swap(dy_wide)

    x, dy_wide, dy_other = lax.optimization_barrier((x, dy_wide, dy_other))
    n1 = norm(x.astype(F32))[0]
    h1 = dot(n1.astype(BF), e_rel).astype(BF)
    cos, sin = rotary_tables(seg)
    qkr, values, pb, att_p, mixed, h2p = kernel_call(
        forward_kernel,
        [((256, QK), BF), ((256, 384), BF), ((H, 256, 256), BF), ((256, 1024), BF),
         ((256, D), F32), ((256, 1024), BF)],
        [((256, D), BF)],
        32,
        4 * 10**9,
        x, h1, *w_at, e_rel, e_abs, cos, sin, seg[:, None], seg[None, :],
    )

    h2_other = swap(h2p)
    w_ff = lax.optimization_barrier((w_ff, h2p))[0]
    m_d = unpack_down(w_ff[:, FF:].reshape(16, 64, 1280))
    kept = lax.dynamic_slice_in_dim(m_d, core * 8, 8, 0)
    came = swap(lax.dynamic_slice_in_dim(m_d, (1 - core) * 8, 8, 0))
    w_d = jnp.stack(by_flag(core == 0, kept, came), axis=1).reshape(1280, 1024)

    d_gu, g_d, y, y_other, h2t = ffn_call(h2p, h2_other, dy_wide, dy_other, w_ff, w_d)
    g_d = g_d.reshape(8, 2, 80, 1024)
    kept = lax.dynamic_index_in_dim(g_d, core, 1, keepdims=False)
    came = swap(lax.dynamic_index_in_dim(g_d, 1 - core, 1, keepdims=False))
    g_d = pack_down(jnp.concatenate(by_flag(core == 0, kept, came), axis=0)).reshape(1024, 1280)
    g_ff, e_own, e_other = ffn_grad_call(h2t, d_gu, w_ff)
    g_ff = lax.dynamic_update_slice(g_ff, g_d, (0, FF))
    t_ff = lax.psum_scatter(g_ff, "shard", scatter_dimension=0, tiled=True)
    out = (mixed + y[:, :D] + swap(y_other.astype(BF)).astype(F32)[:, :D]).astype(BF)

    grad_in, g_own, g_other = kernel_call(
        backward_kernel,
        [((256, D), BF), ((512, 2 * QK), BF), ((512, 2 * QK), BF)],
        [((256, D), BF), ((256, QK), F32), ((256, QK), BF), ((256, QK), BF), ((256, QK), BF),
         ((256, D), F32)],
        48,
        8 * 10**9,
        e_own, swap(e_other), dy, mixed, h1, att_p, qkr, values, pb, *w_at,
        e_rel, e_abs, cos, sin, x,
    )
    t_at = scatter_rel(g_own, g_other, where)
    t_at = jnp.concatenate(by_flag(core == 0, t_at, swap(t_at)), axis=0)[:60].astype(F32)

    t_ff = sum_x(t_ff, where)
    t_ff = by_flag(core == 0, t_ff, swap(t_ff))
    columns = lambda at: jnp.concatenate(
        [t[:60, at + 512 * j : at + 512 * j + 256] for t in t_ff for j in range(5)], axis=1
    ).astype(F32)
    t_g, t_u = (columns(0), columns(256))
    t_d = jnp.concatenate([unpack_down(t[None, :, FF:])[0, :, :D] for t in t_ff], axis=0)
    t_q, t_k, t_o, t_v = (t_at[:, :D], t_at[:, D:QK], t_at[:, QK : QK + D], t_at[:, QK + D :])
    rowsum = lambda w, t: jnp.sum(w.astype(F32) * t, axis=1)
    grad_ga = rowsum(wq, t_q) + rowsum(wk, t_k) + rowsum(wv, t_v)
    grad_gf = rowsum(wg, t_g) + rowsum(wu, t_u)
    return (
        out,
        grad_in,
        t_q * ga,
        t_k * ga,
        t_v * ga,
        t_o,
        t_g * gf,
        t_u * gf,
        t_d.astype(F32),
        grad_ga,
        grad_gf,
    )


def solution(mesh):
    token = P(("rep", "shard"), None)
    row = P("shard", None)
    return jax.shard_map(
        local,
        mesh=mesh,
        in_specs=(token, P(("rep", "shard")), token) + (row,) * 7 + (P("shard"),) * 2,
        out_specs=(token, token) + (row,) * 7 + (P("shard"),) * 2,
        check_vma=False,
    )
```

```python
import jax
import jax.numpy as jnp
from jax import lax
from jax.experimental import pallas as pl
from jax.experimental.pallas import tpu as pltpu
from jax.sharding import PartitionSpec as P

H = 15
KVH = 5
HD = 64
D = 960
QK = 1280
FF = 2560
EPSILON = 1e-05
THETA = 100000.0
F32 = jnp.float32
BF = jnp.bfloat16
AX = ("rep", "shard")


def device(x, c, z, y):
    return ((x % 4) * 2 + c % 2) * 16 + (z % 4) * 4 + y % 4


def shift(value, axis, step):
    move = {"x": 0, "c": 0, "z": 0, "y": 0, axis: step}
    pairs = [
        (device(x, c, z, y), device(x + move["x"], c + move["c"], z + move["z"], y + move["y"]))
        for x in range(4)
        for c in range(2)
        for z in range(4)
        for y in range(4)
    ]
    return lax.ppermute(value, AX, pairs)


def dot(left, right):
    return jnp.dot(left, right, preferred_element_type=F32)


def dot_t(left, right):
    return lax.dot_general(left, right, (((1,), (1,)), ((), ())), preferred_element_type=F32)


def t_dot(left, right):
    return lax.dot_general(left, right, (((0,), (0,)), ((), ())), preferred_element_type=F32)


def collect(value, axis):
    return [value] + [shift(value, axis, -step) for step in (1, 2, 3)]


def spread(blocks, axis):
    got = [shift(blocks[step], axis, step) for step in (1, 2, 3)]
    total = blocks[0].astype(F32)
    for part in got:
        total = total + part.astype(F32)
    return total.astype(BF)


def place_x(blocks, where, axis):
    size = blocks[0].shape[axis]
    shape = [n * 4 if i == axis else n for i, n in enumerate(blocks[0].shape)]
    whole = jnp.zeros(shape, BF)
    for step, block in enumerate(blocks):
        start = [0] * len(shape)
        start[axis] = (where["x"] + step) % 4 * size
        whole = lax.dynamic_update_slice(whole, block, start)
    return whole


def parts_x(value, where, axis):
    size = value.shape[axis] // 4
    return [
        lax.dynamic_slice_in_dim(value, (where["x"] + step) % 4 * size, size, axis)
        for step in range(4)
    ]


def gather_rel(value, first, second):
    inner = jnp.concatenate(collect(value, first), axis=0)
    mine = jnp.concatenate(collect(inner, second), axis=0)
    return [mine, swap(mine)]


def scatter_rel(own, other, where):
    total = (own.astype(F32) + swap(other).astype(F32)).astype(BF)
    total = spread(parts_x(total, where, 1), "x")
    for axis in ("z", "y"):
        rows = total.shape[0] // 4
        total = spread([total[i * rows : (i + 1) * rows] for i in range(4)], axis)
    return place_x(collect(total, "x"), where, 1)


def swap(value):
    return shift(value, "c", 1)


def sum_x(part, where):
    return place_x(collect(spread(parts_x(part, where, 0), "x"), "x"), where, 0)


def by_flag(low, mine, other):
    return (jnp.where(low, mine, other), jnp.where(low, other, mine))


def pack_down(value):
    last = value[:, 64:]
    tail = jnp.concatenate([last[:, :, i * 256 : (i + 1) * 256] for i in range(4)], axis=1)
    return jnp.concatenate([value[:, :64], tail], axis=2)


def unpack_down(value):
    tail = value[:, :, 1024:]
    last = jnp.concatenate([tail[:, i * 16 : (i + 1) * 16] for i in range(4)], axis=2)
    return jnp.concatenate([value[:, :, :1024], last], axis=1)


def order_rel(where, major, minor):
    place = lax.broadcasted_iota(jnp.int32, (D, 1024), 1)
    natural = lax.broadcasted_iota(jnp.int32, (D, 1024), 0)
    core = (where["c"] + place // 512) % 2
    at = {
        major: (where[major] + (place // 128) % 4) % 4,
        minor: (where[minor] + (place // 32) % 4) % 4,
    }
    inner = core * 32 + place % 32
    return (((at["z"] * 4 + at["y"]) * 60 + inner == natural) & (inner < 60)).astype(BF)


def order_abs():
    place = lax.broadcasted_iota(jnp.int32, (D, 1024), 1)
    natural = lax.broadcasted_iota(jnp.int32, (D, 1024), 0)
    inner = place % 64
    return (((place // 64) * 60 + inner == natural) & (inner < 60)).astype(BF)


def rotary_tables(segments):
    count = segments.shape[0]
    index = jnp.arange(count, dtype=jnp.int32)
    same = segments[:, None] == segments[None, :]
    first = jnp.min(jnp.where(same, index[None, :], count), axis=-1)
    position = (index - first).astype(F32)
    half = HD // 2
    freq = THETA ** (-jnp.arange(half, dtype=F32) / half)
    angle = position[:, None] * freq
    cos, sin = (jnp.cos(angle), jnp.sin(angle))
    return (
        jnp.concatenate([cos] * 4, axis=1),
        jnp.concatenate([-sin, sin, -sin, sin], axis=1),
    )


def norm(values):
    scale = lax.rsqrt(jnp.mean(values * values, axis=-1, keepdims=True) + EPSILON)
    return (values * scale, scale)


def norm_back(e, normed, scale):
    return scale * (e - normed * jnp.mean(e * normed, axis=-1, keepdims=True))


def swap_halves(block):
    lane = lax.broadcasted_iota(jnp.int32, block.shape, 1)
    return jnp.where(lane % 64 < 32, pltpu.roll(block, 96, 1), pltpu.roll(block, 32, 1))


def forward_kernel(
    x_ref, h1a_ref, h1b_ref, wqk_ref, wqk2_ref, wov_ref, wov2_ref, ea_ref, eb_ref, eabs_ref, cos_ref, sin_ref, segc_ref,
    segr_ref,
    qkr_ref, v_ref, pb_ref, attp_ref, mixed_ref, h2p_ref, att_ref,
):
    cos, sin = (cos_ref[...], sin_ref[...])
    for i in range(10):
        lanes = slice(128 * i, 128 * i + 128)
        part = dot(h1a_ref[:, :512], wqk_ref[:, lanes]) + dot(h1a_ref[:, 512:], wqk2_ref[:, lanes])
        qkr_ref[:, lanes] = (part * cos + swap_halves(part) * sin).astype(BF)
    v_ref[...] = (
        dot(h1b_ref[:, :512], wov_ref[:, 896:]) + dot(h1b_ref[:, 512:], wov2_ref[:, 896:])
    ).astype(BF)
    row = lax.broadcasted_iota(jnp.int32, (256, 256), 0)
    col = lax.broadcasted_iota(jnp.int32, (256, 256), 1)
    allowed = (segc_ref[...] == segr_ref[...]) & (row >= col)
    for h in range(H):
        g = h // 3
        q = qkr_ref[:, 64 * h : 64 * h + 64]
        k = qkr_ref[:, D + 64 * g : D + 64 * g + 64]
        scores = jnp.where(allowed, dot_t(q, k) * 0.125, -1e30)
        weight = jnp.exp(scores - jnp.max(scores, axis=-1, keepdims=True))
        pb = (weight / jnp.sum(weight, axis=-1, keepdims=True)).astype(BF)
        pb_ref[h] = pb
        att_ref[:, 64 * h : 64 * h + 64] = dot(pb, v_ref[:, 64 + 64 * g : 128 + 64 * g]).astype(BF)
    attp_ref[...] = dot(att_ref[...], ea_ref[...]).astype(BF)
    att_p = dot(att_ref[...], eb_ref[...]).astype(BF)
    mixed = (
        x_ref[...].astype(F32)
        + dot(att_p[:, :512], wov_ref[:, :D])
        + dot(att_p[:, 512:], wov2_ref[:, :D])
    )
    mixed_ref[...] = mixed
    h2p_ref[...] = dot(norm(mixed)[0].astype(BF), eabs_ref[...]).astype(BF)


def ffn_kernel(
    h2a_ref, h2b_ref, dya_ref, dyb_ref, wg_ref, wu_ref, wd_ref,
    dgu_ref, gd_ref, ya_ref, yb_ref, h2t_ref, h2_ref, dy_ref,
):
    @pl.when(pl.program_id(0) == 0)
    def _():
        h2_ref[:256] = h2a_ref[...]
        h2_ref[256:] = h2b_ref[...]
        dy_ref[:256] = dya_ref[...]
        dy_ref[256:] = dyb_ref[...]
        h2t_ref[...] = h2_ref[...].T
        ya_ref[...] = jnp.zeros_like(ya_ref)
        yb_ref[...] = jnp.zeros_like(yb_ref)

    h2, dy, wd = (h2_ref[...], dy_ref[...], wd_ref[...])
    gate, up, d_act = (dot(h2, wg_ref[...]), dot(h2, wu_ref[...]), dot_t(dy, wd))
    sig = jax.nn.sigmoid(gate)
    silu = gate * sig
    act = (silu * up).astype(BF)
    dgu_ref[:, :256] = (d_act * up * sig * (1.0 + gate * (1.0 - sig))).astype(BF)
    dgu_ref[:, 256:] = (d_act * silu).astype(BF)
    gd_ref[...] = dot(act.T, dy).astype(BF)
    ya_ref[...] += dot(act[:256], wd)
    yb_ref[...] += dot(act[256:], wd)


def ffn_grad_kernel(h2t_ref, dgu_ref, wg_ref, wu_ref, gg_ref, ea_ref, eb_ref, total_ref):
    j = pl.program_id(0)

    @pl.when(j == 0)
    def _():
        total_ref[...] = jnp.zeros_like(total_ref)

    dgu = dgu_ref[...]
    gg_ref[...] = dot(h2t_ref[...], dgu).astype(BF)
    total_ref[...] += dot_t(dgu[:, :256], wg_ref[...]) + dot_t(dgu[:, 256:], wu_ref[...])

    @pl.when(j == 4)
    def _():
        ea_ref[...] = total_ref[:256]
        eb_ref[...] = total_ref[256:].astype(BF)


def backward_kernel(
    ef_ref, came_ref, dy_ref, mixed_ref, h1_ref, attp_ref, qkr_ref, v_ref, pb_ref,
    wqk_ref, wqk2_ref, wov_ref, wov2_ref, ea_ref, eb_ref, eabs_ref, cos_ref, sin_ref, x_ref,
    gin_ref, own_ref, other_ref,
    dob_ref, raw_ref, da_ref, dqk_ref, dv_ref, dmixed_ref,
):
    e = dot_t((ef_ref[...] + came_ref[...].astype(F32)).astype(BF), eabs_ref[...])
    n2, r2 = norm(mixed_ref[...])
    d_mixed = dy_ref[...].astype(F32) + norm_back(e, n2, r2)
    dmixed_ref[...] = d_mixed
    d_attn = d_mixed.astype(BF)
    da_ref[:, :D] = d_attn
    da_ref[:, D:] = jnp.zeros((256, 320), BF)
    dob_ref[...] = (
        dot_t(dot_t(d_attn, wov_ref[:, :D]).astype(BF), eb_ref[:, :512])
        + dot_t(dot_t(d_attn, wov2_ref[:, :D]).astype(BF), eb_ref[:, 512:])
    ).astype(BF)
    dv_ref[:, :D] = jnp.zeros((256, D), BF)
    for g in range(KVH):
        k = qkr_ref[:, D + 64 * g : D + 64 * g + 64]
        v = v_ref[:, 64 + 64 * g : 128 + 64 * g]
        d_v = jnp.zeros((256, HD), F32)
        d_k = jnp.zeros((256, HD), F32)
        for h in range(3 * g, 3 * g + 3):
            pb = pb_ref[h]
            d_ob = dob_ref[:, 64 * h : 64 * h + 64]
            d_p = dot_t(d_ob, v)
            probs = pb.astype(F32)
            row_dot = jnp.sum(probs * d_p, axis=-1, keepdims=True)
            d_s = (probs * (d_p - row_dot) * 0.125).astype(BF)
            raw_ref[:, 64 * h : 64 * h + 64] = dot(d_s, k)
            d_v += t_dot(pb, d_ob)
            d_k += t_dot(d_s, qkr_ref[:, 64 * h : 64 * h + 64])
        raw_ref[:, D + 64 * g : D + 64 * g + 64] = d_k
        dv_ref[:, D + 64 * g : D + 64 * g + 64] = d_v.astype(BF)
    cos, sin = (cos_ref[...], sin_ref[...])
    for i in range(10):
        lanes = slice(128 * i, 128 * i + 128)
        part = raw_ref[:, lanes]
        dqk_ref[:, lanes] = (part * cos - swap_halves(part) * sin).astype(BF)
    for ref, rows in ((other_ref, slice(512, 1024)), (own_ref, slice(0, 512))):
        h1t = h1_ref[:, rows].T
        ref[:, :QK] = dot(h1t, dqk_ref[...]).astype(BF)
        ref[:, QK:] = (dot(attp_ref[:, rows].T, da_ref[...]) + dot(h1t, dv_ref[...])).astype(BF)
    e = 0.0
    for qk_ref, ov_ref, rows in (
        (wqk_ref, wov_ref, slice(0, 512)),
        (wqk2_ref, wov2_ref, slice(512, 1024)),
    ):
        part = dot_t(dqk_ref[...], qk_ref[...]).astype(BF)
        e = e + dot_t(part, ea_ref[:, rows])
        part = dot_t(dv_ref[:, 896:], ov_ref[:, 896:]).astype(BF)
        e = e + dot_t(part, eb_ref[:, rows])
    n1, r1 = norm(x_ref[...].astype(F32))
    gin_ref[...] = (dmixed_ref[...] + norm_back(e, n1, r1)).astype(BF)


def in_hbm(value):
    return pltpu.with_memory_space_constraint(value, pltpu.HBM)


def kernel_call(kernel, outs, scratch, mib, flops, *args):
    spec = lambda a: pl.BlockSpec(
        a.shape, lambda i: (0,) * len(a.shape), pipeline_mode=pl.Buffered(1)
    )
    shapes = [jax.ShapeDtypeStruct(*out) for out in outs]
    size = sum(s.size * s.dtype.itemsize for s in list(args) + shapes)
    return pl.pallas_call(
        kernel,
        grid=(1,),
        out_shape=[pltpu.HBM(*out) for out in outs],
        in_specs=[spec(a) for a in args],
        out_specs=[spec(a) for a in shapes],
        scratch_shapes=[pltpu.VMEM(*s) for s in scratch],
        compiler_params=pltpu.CompilerParams(vmem_limit_bytes=mib * 2**20),
        cost_estimate=pl.CostEstimate(flops=flops, bytes_accessed=size, transcendentals=0),
    )(*[in_hbm(a) for a in args])


def ffn_call(h2a, h2b, dya, dyb, w_ff, w_d):
    fixed = lambda j: (0, 0)
    token = pl.BlockSpec((256, 1024), fixed)
    return pl.pallas_call(
        ffn_kernel,
        grid=(5,),
        out_shape=[
            pltpu.HBM((512, 2560), BF),
            jax.ShapeDtypeStruct((1280, 1024), BF),
            pltpu.HBM((256, 1024), F32),
            pltpu.HBM((256, 1024), F32),
            pltpu.HBM((1024, 512), BF),
        ],
        in_specs=[token] * 4
        + [
            pl.BlockSpec((1024, 256), lambda j: (0, j)),
            pl.BlockSpec((1024, 256), lambda j: (0, 5 + j)),
            pl.BlockSpec((256, 1024), lambda j: (j, 0)),
        ],
        out_specs=[
            pl.BlockSpec((512, 512), lambda j: (0, j)),
            pl.BlockSpec((256, 1024), lambda j: (j, 0)),
            token,
            token,
            pl.BlockSpec((1024, 512), fixed),
        ],
        scratch_shapes=[pltpu.VMEM((512, 1024), BF), pltpu.VMEM((512, 1024), BF)],
        compiler_params=pltpu.CompilerParams(vmem_limit_bytes=22 * 2**20),
        cost_estimate=pl.CostEstimate(
            flops=7 * 10**9, bytes_accessed=20 * 10**6, transcendentals=512 * 1280
        ),
    )(in_hbm(h2a), in_hbm(h2b), in_hbm(dya), in_hbm(dyb), in_hbm(w_ff), in_hbm(w_ff), w_d)


def ffn_grad_call(h2t, dgu, w_ff):
    fixed = lambda j: (0, 0)
    token = pl.BlockSpec((256, 1024), fixed)
    return pl.pallas_call(
        ffn_grad_kernel,
        grid=(5,),
        out_shape=[
            pltpu.HBM((1024, 3840), BF),
            pltpu.HBM((256, 1024), F32),
            pltpu.HBM((256, 1024), BF),
        ],
        in_specs=[
            pl.BlockSpec((1024, 512), fixed),
            pl.BlockSpec((512, 512), lambda j: (0, j)),
            pl.BlockSpec((1024, 256), lambda j: (0, j)),
            pl.BlockSpec((1024, 256), lambda j: (0, 5 + j)),
        ],
        out_specs=[pl.BlockSpec((1024, 512), lambda j: (0, j)), token, token],
        scratch_shapes=[pltpu.VMEM((512, 1024), F32)],
        compiler_params=pltpu.CompilerParams(vmem_limit_bytes=18 * 2**20),
        cost_estimate=pl.CostEstimate(
            flops=6 * 10**9, bytes_accessed=16 * 10**6, transcendentals=0
        ),
    )(in_hbm(h2t), in_hbm(dgu), in_hbm(w_ff), in_hbm(w_ff))


def local(x, seg, dy, wq, wk, wv, wo, wg, wu, wd, gain_a, gain_f):
    rep = lax.axis_index("rep")
    shard = lax.axis_index("shard")
    where = {"x": rep // 2, "c": rep % 2, "z": shard // 4, "y": shard % 4}
    core = where["c"]
    ga = gain_a[:, None]
    gf = gain_f[:, None]
    scaled = lambda w, g: (w.astype(F32) * g).astype(BF)
    tall = lambda w: jnp.pad(w, ((0, 4), (0, 0)))
    s_at = tall(jnp.concatenate([scaled(wq, ga), scaled(wk, ga), wo, scaled(wv, ga)], axis=1))
    s_at = lax.dynamic_slice_in_dim(s_at, core * 32, 32, 0)
    w_qk = gather_rel(s_at[:, :QK], "y", "z")
    w_ov = gather_rel(s_at[:, QK:], "z", "y")
    half = lambda w: lax.dynamic_slice_in_dim(w, core * 1280, 1280, 1)
    s_d = jnp.pad(lax.dynamic_slice_in_dim(wd, core * 80, 80, 0), ((0, 0), (0, 64)))
    s_ff = jnp.concatenate(
        [tall(scaled(half(wg), gf)), tall(scaled(half(wu), gf)), pack_down(s_d[None])[0]], axis=1
    )
    w_ff = lax.all_gather(s_ff, "shard", axis=0, tiled=True)
    e_a = order_rel(where, "z", "y")
    e_b = order_rel(where, "y", "z")
    e_abs = order_abs()
    dy_wide = jnp.pad(dy, ((0, 0), (0, 64)))
    dy_other = swap(dy_wide)

    x, dy_wide, dy_other = lax.optimization_barrier((x, dy_wide, dy_other))
    n1 = norm(x.astype(F32))[0]
    h1a = dot(n1.astype(BF), e_a).astype(BF)
    h1b = dot(n1.astype(BF), e_b).astype(BF)
    cos, sin = rotary_tables(seg)
    qkr, values, pb, att_p, mixed, h2p = kernel_call(
        forward_kernel,
        [((256, QK), BF), ((256, 384), BF), ((H, 256, 256), BF), ((256, 1024), BF),
         ((256, D), F32), ((256, 1024), BF)],
        [((256, D), BF)],
        32,
        4 * 10**9,
        x, h1a, h1b, *w_qk, *w_ov, e_a, e_b, e_abs, cos, sin, seg[:, None], seg[None, :],
    )

    h2_other = swap(h2p)
    w_ff = lax.optimization_barrier((w_ff, h2p))[0]
    m_d = unpack_down(w_ff[:, FF:].reshape(16, 64, 1280))
    kept = lax.dynamic_slice_in_dim(m_d, core * 8, 8, 0)
    came = swap(lax.dynamic_slice_in_dim(m_d, (1 - core) * 8, 8, 0))
    w_d = jnp.stack(by_flag(core == 0, kept, came), axis=1).reshape(1280, 1024)

    d_gu, g_d, y, y_other, h2t = ffn_call(h2p, h2_other, dy_wide, dy_other, w_ff, w_d)
    g_d = g_d.reshape(8, 2, 80, 1024)
    kept = lax.dynamic_index_in_dim(g_d, core, 1, keepdims=False)
    came = swap(lax.dynamic_index_in_dim(g_d, 1 - core, 1, keepdims=False))
    g_d = pack_down(jnp.concatenate(by_flag(core == 0, kept, came), axis=0)).reshape(1024, 1280)
    g_ff, e_own, e_other = ffn_grad_call(h2t, d_gu, w_ff)
    g_ff = lax.dynamic_update_slice(g_ff, g_d, (0, FF))
    t_ff = lax.psum_scatter(g_ff, "shard", scatter_dimension=0, tiled=True)
    out = (mixed + y[:, :D] + swap(y_other.astype(BF)).astype(F32)[:, :D]).astype(BF)

    grad_in, g_own, g_other = kernel_call(
        backward_kernel,
        [((256, D), BF), ((512, 2 * QK), BF), ((512, 2 * QK), BF)],
        [((256, D), BF), ((256, QK), F32), ((256, QK), BF), ((256, QK), BF), ((256, QK), BF),
         ((256, D), F32)],
        48,
        8 * 10**9,
        e_own, swap(e_other), dy, mixed, h1a, att_p, qkr, values, pb, *w_qk,
        *w_ov, e_a, e_b, e_abs, cos, sin, x,
    )
    t_at = scatter_rel(g_own, g_other, where)
    t_at = jnp.concatenate(by_flag(core == 0, t_at, swap(t_at)), axis=0)[:60].astype(F32)

    t_ff = sum_x(t_ff, where)
    t_ff = by_flag(core == 0, t_ff, swap(t_ff))
    columns = lambda at: jnp.concatenate(
        [t[:60, at + 512 * j : at + 512 * j + 256] for t in t_ff for j in range(5)], axis=1
    ).astype(F32)
    t_g, t_u = (columns(0), columns(256))
    t_d = jnp.concatenate([unpack_down(t[None, :, FF:])[0, :, :D] for t in t_ff], axis=0)
    t_q, t_k, t_o, t_v = (t_at[:, :D], t_at[:, D:QK], t_at[:, QK : QK + D], t_at[:, QK + D :])
    rowsum = lambda w, t: jnp.sum(w.astype(F32) * t, axis=1)
    grad_ga = rowsum(wq, t_q) + rowsum(wk, t_k) + rowsum(wv, t_v)
    grad_gf = rowsum(wg, t_g) + rowsum(wu, t_u)
    return (
        out,
        grad_in,
        t_q * ga,
        t_k * ga,
        t_v * ga,
        t_o,
        t_g * gf,
        t_u * gf,
        t_d.astype(F32),
        grad_ga,
        grad_gf,
    )


def solution(mesh):
    token = P(("rep", "shard"), None)
    row = P("shard", None)
    return jax.shard_map(
        local,
        mesh=mesh,
        in_specs=(token, P(("rep", "shard")), token) + (row,) * 7 + (P("shard"),) * 2,
        out_specs=(token, token) + (row,) * 7 + (P("shard"),) * 2,
        check_vma=False,
    )
```
